32 devices in a mesh: groups: 2 (over x), seq: 16 (over z, y, core).
Axes of the slice: x: 2, y: 2, z: 4, core: 2. Of those that a mesh axis runs over, the one named last changes fastest.
Arguments:
- tokens: bfloat16 [8192, 4096], P(('groups', 'seq')), parts along dimension 0, may hold values from -14 to 14, as said below
- norm_gain: float32 [4096], replicated, may hold values from 0.25 to 1.75
- w_query: bfloat16 [4096, 2048], P('seq'), may hold values from -1 to 1, as said below
- w_key: bfloat16 [4096, 512], P('seq'), may hold values from -24 to 24
- w_value: bfloat16 [4096, 512], P('seq'), may hold values from -0.09375 to 0.09375
- passage_blocks: int32 [64], P(('groups', 'seq')), parts along dimension 0, may hold values from 0 to 9, as said below
Outputs:
- attended: bfloat16 [8192, 2048], P(('groups', 'seq')), parts along dimension 0
The draws below stay inside these ranges and needn't reach their ends.
There are 2 independent parts, one for each index of `groups`. The reference program is written for one: setup_inputs(seed, part) draws one part's arguments, and reference() takes and returns one part's arrays. A program takes and returns all parts, laid end to end along the dimension named above; an argument that names none is the same for every part. Nothing has to cross between parts.
Inputs may be any that keep to these rules, and one draw needn't show every extreme that they name: `passage_blocks`: passage numbers never fall along the row; each passage covers 1 to 7 whole blocks; the first and the last passage of the row cover exactly 7. `tokens`: hidden states of order one. `w_query`: entries of order 4096 ** -0.5.
All inputs are finite; a program needn't handle non-finite values.
Results may differ from the reference program's by a relative error of at most 0.0049.
The reference program's roundings to bfloat16 on the way (of `normed`, `query` and `rounded`) count: a program that leaves them out, or rounds other values in their place, can miss the bound.
Values may be sent and summed in bfloat16 or wider, within the bound.
No kernel may reach another device: no remote copies, remote signals or barrier semaphores. Data moves between devices by JAX's collectives and lax.ppermute only.
A program may use at most 128 MiB of HBM per device.

```python
import jax
import jax.numpy as jnp
from jax import lax

D = 4096
HD = 128
QH = 16
KVH = 4
BLOCK = 128
REACH = 3
TOK_DEV = 256
NBLK = 32
TOKENS = 4096
MOST_BLK = 7
PASSAGES = 10
N_SEQ = 16


def query_matrix(key):
    sample = jax.random.normal(jax.random.fold_in(key, 11), (D, QH * HD), jnp.float32)
    return jnp.clip(sample, -6.0, 6.0) * D ** (-0.5)


def draw_w_query(key, part):
    return query_matrix(key).astype(jnp.bfloat16)


def draw_w_key(key, part):
    jitter = jnp.clip(jax.random.normal(jax.random.fold_in(key, 12), (D, KVH * HD), jnp.float32), -6.0, 6.0) * D ** (-0.5)
    return jitter.astype(jnp.bfloat16)


def draw_tokens(key, part):
    sample = jax.random.normal(jax.random.fold_in(key, 23), (TOKENS, D), jnp.float32)
    return jnp.clip(sample, -6.0, 6.0).astype(jnp.bfloat16)


def draw_passage_blocks(key, part):
    middle_blocks = NBLK - 2 * MOST_BLK
    middle_count = PASSAGES - 2
    extra_total = middle_blocks - middle_count
    slots = middle_count * (MOST_BLK - 1)
    order = jax.random.permutation(jax.random.fold_in(key, 31), slots)
    owners = (order[:extra_total] // (MOST_BLK - 1)).astype(jnp.int32)
    labels = jnp.arange(middle_count, dtype=jnp.int32)
    extra = jnp.sum((owners[:, None] == labels[None, :]).astype(jnp.int32), axis=0)
    lengths = 1 + extra
    ends = jnp.cumsum(lengths).astype(jnp.int32)
    positions = jnp.arange(middle_blocks, dtype=jnp.int32)
    middle_ids = 1 + jnp.sum((positions[:, None] >= ends[None, :]).astype(jnp.int32), axis=1)
    head_ids = jnp.zeros((MOST_BLK,), jnp.int32)
    tail_ids = jnp.full((MOST_BLK,), PASSAGES - 1, jnp.int32)
    return jnp.concatenate([head_ids, middle_ids.astype(jnp.int32), tail_ids]).astype(jnp.int32)


def level_of(stream_key, extent, cuts, low, largest):
    gain = 1.0
    for position, parts in cuts:
        draws = jax.random.uniform(jax.random.fold_in(jax.random.fold_in(stream_key, 6), position), (parts,), jnp.float32, low / len(cuts), largest / len(cuts))
        gain = gain * jnp.repeat(jnp.exp(draws), extent[position] // parts).reshape((-1,) + (1,) * (len(extent) - 1 - position))
    return gain


def scatter_about(stream_key, shape, deviation, reach, shards=(), kind=jnp.bfloat16):
    drawn = jax.random.normal(stream_key, shape, jnp.float32) * deviation
    if len(shards) > 0:
        drawn = level_of(stream_key, shape, shards, -0.22, 0.18) * drawn
    return jnp.clip(drawn, min=-reach, max=reach).astype(kind)


def setup_inputs(seed: int = 0, part: int = 0) -> dict:
    key_of = jax.random.split(jax.random.key(seed), 7)
    own_keys = jax.random.split(jax.random.fold_in(key_of[6], part), 7)
    return {
        "tokens": draw_tokens(jax.random.fold_in(jax.random.fold_in(key_of[6], part), 71), part),
        "norm_gain": jnp.clip(1.0 + 0.15 * jax.random.normal(key_of[1], (D,), jnp.float32), 0.25, 1.75),
        "w_query": draw_w_query(jax.random.fold_in(key_of[6], 71), part),
        "w_key": draw_w_key(jax.random.fold_in(key_of[6], 71), part),
        "w_value": scatter_about(key_of[4], (D, KVH * HD), D ** -0.5, 0.09375, ((0, 16),)),
        "passage_blocks": draw_passage_blocks(jax.random.fold_in(jax.random.fold_in(key_of[6], part), 71), part),
    }


def normalize(tokens, norm_gain):
    widened = tokens.astype(jnp.float32)
    inverse = lax.rsqrt(lax.optimization_barrier(jnp.mean(widened * widened, axis=-1, keepdims=True)) + 1e-05)
    return (widened * inverse * norm_gain).astype(jnp.bfloat16)

def attend_window(query, keys, values, query_ids, key_ids):
    row_count = query.shape[0]
    key_count = keys.shape[0]
    group = QH // KVH
    query_heads = query.reshape(row_count, KVH, group, HD).transpose(1, 0, 2, 3)
    key_heads = keys.reshape(key_count, KVH, HD).transpose(1, 0, 2)
    value_heads = values.reshape(key_count, KVH, HD).transpose(1, 0, 2)
    allowed = query_ids[:, None] == key_ids[None, :]

    def one_head(operands):
        head_query, head_keys, head_values = operands
        scores = jnp.einsum('tgd,sd->gts', head_query.astype(jnp.float32), head_keys.astype(jnp.float32)) * HD ** (-0.5)
        scores = jnp.where(allowed[None], scores, -1e+30)
        row_max = lax.optimization_barrier(jnp.max(scores, axis=-1, keepdims=True))
        weights = jnp.exp(scores - row_max)
        row_total = lax.optimization_barrier(jnp.sum(weights, axis=-1, keepdims=True))
        rounded = lax.optimization_barrier(weights.astype(jnp.bfloat16))
        mixed = jnp.einsum('gts,sd->tgd', rounded.astype(jnp.float32), head_values.astype(jnp.float32))
        return mixed / row_total.transpose(1, 0, 2)
    stacked = lax.map(one_head, (query_heads, key_heads, value_heads))
    return stacked.transpose(1, 0, 2, 3).reshape(row_count, QH * HD)

def reference(tokens, norm_gain, w_query, w_key, w_value, passage_blocks):
    normed = normalize(tokens, norm_gain)
    query = jnp.dot(normed, w_query, preferred_element_type=jnp.float32).astype(jnp.bfloat16)
    keys = jnp.dot(normed, w_key, preferred_element_type=jnp.float32).astype(jnp.bfloat16)
    values = jnp.dot(normed, w_value, preferred_element_type=jnp.float32).astype(jnp.bfloat16)
    passage = jnp.repeat(passage_blocks + 1, BLOCK).astype(jnp.int32)
    margin = REACH * TOK_DEV
    keys_wide = jnp.pad(keys, ((margin, margin), (0, 0)))
    values_wide = jnp.pad(values, ((margin, margin), (0, 0)))
    passage_wide = jnp.pad(passage, (margin, margin))
    window_len = (2 * REACH + 1) * TOK_DEV

    def one_shard(index):
        first_row = (index * TOK_DEV).astype(jnp.int32)
        shard_query = lax.dynamic_slice_in_dim(query, first_row, TOK_DEV, 0)
        shard_ids = lax.dynamic_slice_in_dim(passage, first_row, TOK_DEV, 0)
        near_keys = lax.dynamic_slice_in_dim(keys_wide, first_row, window_len, 0)
        near_values = lax.dynamic_slice_in_dim(values_wide, first_row, window_len, 0)
        near_ids = lax.dynamic_slice_in_dim(passage_wide, first_row, window_len, 0)
        return attend_window(shard_query, near_keys, near_values, shard_ids, near_ids).astype(jnp.bfloat16)
    result = lax.map(one_shard, jnp.arange(N_SEQ, dtype=jnp.int32))
    return result.reshape(TOKENS, QH * HD)
```

```python
import functools

import jax
import jax.numpy as jnp
from jax import lax
from jax.experimental import pallas as pl
from jax.experimental.pallas import tpu as pltpu
from jax.sharding import PartitionSpec as P

HD = 128
MOST_BLK = 7
LANES = 128
AXES = ("groups", "seq")
VMEM_LIMIT = 56 * 1024 * 1024


def normalize(tokens, norm_gain):
    widened = tokens.astype(jnp.float32)
    inverse = lax.rsqrt(jnp.mean(widened * widened, axis=-1, keepdims=True) + 1e-05)
    return (widened * inverse * norm_gain).astype(jnp.bfloat16)


def swap(value, team, group_bits, layer_bits, member_bits):
    groups, peers = lax.axis_size("groups"), lax.axis_size("seq")
    pairs = []
    for g in range(groups):
        for s in range(peers):
            layer, member = divmod(s, team)
            to = (layer ^ layer_bits) * team + (member ^ member_bits)
            pairs.append((g * peers + s, (g ^ group_bits) * peers + to))
    return lax.ppermute(value, AXES, pairs)


def from_layer(value, team, by):
    groups, peers = lax.axis_size("groups"), lax.axis_size("seq")
    pairs = []
    for g in range(groups):
        for s in range(peers):
            to = s - by * team
            if 0 <= to < peers:
                pairs.append((g * peers + s, g * peers + to))
    return lax.ppermute(value, AXES, pairs)


def gather_columns(blocks, team, place):
    groups = lax.axis_size("groups")
    layers = lax.axis_size("seq") // team
    group = place[0]
    depth = blocks[0].shape[0]
    part = depth // groups

    def share(value):
        return lax.dynamic_slice_in_dim(value, group * part, part, 0)

    near = swap(blocks[1], team, 0, 0, 1)
    far = [swap(share(blocks[r]), team, 0, 0, r) for r in range(2, team)]
    far = jnp.concatenate(far, axis=0)
    held = {(0, 0): jnp.concatenate([share(blocks[0]), share(near), far], axis=0)}
    found = [
        (blocks[0], [(0, 0, None)]),
        (near, [(0, 1, None)]),
        (far, [(0, r, 0) for r in range(2, team)]),
    ]
    for bits in range(1, layers):
        low = bits & -bits
        held[(bits, 0)] = swap(held[(bits ^ low, 0)], team, 0, low, 0)
        found.append((held[(bits, 0)], [(bits, r, 0) for r in range(team)]))
    for other in range(1, groups):
        found.append(
            (swap(far, team, other, 0, 0), [(0, r, other) for r in range(2, team)])
        )
        for bits in range(1, layers):
            moved = swap(held[(bits, 0)], team, other, 0, 0)
            found.append((moved, [(bits, r, other) for r in range(team)]))
    return found


def project_kernel(pieces, team, groups, depth, place, *refs):
    token_refs = refs[:team]
    weight_refs = refs[team : team + len(pieces)]
    out_ref = refs[team + len(pieces)]
    tokens, weights, total, token_sems, weight_sems = refs[team + len(pieces) + 1 :]
    rows = token_refs[0].shape[0]
    part = depth // groups
    group, layer, member = place[0], place[1], place[2]
    token_copies = [
        pltpu.make_async_copy(
            token_refs[t], tokens.at[pl.ds(t * rows, rows)], token_sems.at[t]
        )
        for t in range(team)
    ]
    weight_copies = []
    offset = 0
    spans = []
    for i, ref in enumerate(weight_refs):
        spans.append((offset, ref.shape[0]))
        weight_copies.append(
            pltpu.make_async_copy(
                ref, weights.at[pl.ds(offset, ref.shape[0])], weight_sems.at[i]
            )
        )
        offset += ref.shape[0]
    for copy in token_copies:
        copy.start()
    for copy in weight_copies:
        copy.start()
    for copy in token_copies:
        copy.wait()
    for i, described in enumerate(pieces):
        weight_copies[i].wait()
        columns = []
        for layer_bits, member_bits, group_bits in described:
            owner = (layer ^ layer_bits) * team + (member ^ member_bits)
            first, length = owner * depth, depth
            if group_bits is not None:
                first, length = first + (group ^ group_bits) * part, part
            columns.append(
                tokens[:, pl.ds(pl.multiple_of(first, LANES), length)]
            )
        left = columns[0] if len(columns) == 1 else jnp.concatenate(columns, axis=1)
        start, length = spans[i]
        term = jnp.dot(
            left, weights[pl.ds(start, length), :], preferred_element_type=jnp.float32
        )
        if i == 0:
            total[...] = term
        else:
            total[...] += term
    for t in range(team):
        first = pl.multiple_of((member ^ t) * rows, rows)
        out_ref[pl.ds(first, rows), :] = total[pl.ds(t * rows, rows), :].astype(
            jnp.bfloat16
        )


def project(place, team_tokens, found, groups, depth):
    team = len(team_tokens)
    rows, width = team_tokens[0].shape
    arrays = [array for array, _ in found]
    pieces = [described for _, described in found]
    columns = arrays[0].shape[1]
    kernel = functools.partial(project_kernel, pieces, team, groups, depth)
    return pl.pallas_call(
        kernel,
        out_shape=jax.ShapeDtypeStruct((team * rows, columns), jnp.bfloat16),
        in_specs=[pl.BlockSpec(memory_space=pltpu.SMEM)]
        + [pl.BlockSpec(memory_space=pl.ANY)] * (team + len(arrays)),
        out_specs=pl.BlockSpec(memory_space=pltpu.VMEM),
        scratch_shapes=[
            pltpu.VMEM((team * rows, width), jnp.bfloat16),
            pltpu.VMEM((width, columns), jnp.bfloat16),
            pltpu.VMEM((team * rows, columns), jnp.float32),
            pltpu.SemaphoreType.DMA((team,)),
            pltpu.SemaphoreType.DMA((len(arrays),)),
        ],
        compiler_params=pltpu.CompilerParams(vmem_limit_bytes=VMEM_LIMIT),
        cost_estimate=pl.CostEstimate(
            flops=2 * team * rows * width * columns,
            bytes_accessed=2 * (team * rows * (width + columns) + width * columns),
            transcendentals=0,
        ),
        name="project",
    )(place, *team_tokens, *arrays)


def attend_kernel(heads, most, first_ref, count_ref, q_ref, before, own, after, out_ref,
                  window, sems):
    step = pl.program_id(0)
    block = q_ref.shape[0]

    @pl.when(step == 0)
    def _():
        copies = []
        offset = 0
        for i, ref in enumerate((before, own, after)):
            copies.append(
                pltpu.make_async_copy(
                    ref, window.at[pl.ds(offset, ref.shape[0])], sems.at[i]
                )
            )
            offset += ref.shape[0]
        for copy in copies:
            copy.start()
        for copy in copies:
            copy.wait()

    first = pl.multiple_of(first_ref[step] * block, block)
    keys = window[pl.ds(first, most * block), :HD]
    values = window[pl.ds(first, most * block), HD:]
    column = lax.broadcasted_iota(jnp.int32, (block, most * block), 1)
    allowed = column < count_ref[step] * block
    for h in range(heads):
        query = q_ref[:, h * HD : (h + 1) * HD]
        scores = lax.dot_general(
            query, keys, (((1,), (1,)), ((), ())), preferred_element_type=jnp.float32
        ) * HD ** (-0.5)
        scores = jnp.where(allowed, scores, -1e30)
        weights = jnp.exp(scores - jnp.max(scores, axis=-1, keepdims=True))
        row_total = jnp.sum(weights, axis=-1, keepdims=True)
        mixed = jnp.dot(
            weights.astype(jnp.bfloat16), values, preferred_element_type=jnp.float32
        )
        out_ref[:, h * HD : (h + 1) * HD] = (mixed / row_total).astype(jnp.bfloat16)


def attend(first, count, query, before, own, after, block):
    rows, columns = query.shape
    heads = columns // HD
    span = before.shape[0] + own.shape[0] + after.shape[0]
    return pl.pallas_call(
        functools.partial(attend_kernel, heads, MOST_BLK),
        out_shape=jax.ShapeDtypeStruct((rows, columns), jnp.bfloat16),
        grid_spec=pltpu.PrefetchScalarGridSpec(
            num_scalar_prefetch=2,
            grid=(rows // block,),
            in_specs=[
                pl.BlockSpec((block, columns), lambda i, *_: (i, 0)),
                pl.BlockSpec(memory_space=pl.ANY),
                pl.BlockSpec(memory_space=pl.ANY),
                pl.BlockSpec(memory_space=pl.ANY),
            ],
            out_specs=pl.BlockSpec((block, columns), lambda i, *_: (i, 0)),
            scratch_shapes=[
                pltpu.VMEM((span, own.shape[1]), jnp.bfloat16),
                pltpu.SemaphoreType.DMA((3,)),
            ],
        ),
        compiler_params=pltpu.CompilerParams(vmem_limit_bytes=VMEM_LIMIT),
        cost_estimate=pl.CostEstimate(
            flops=4 * rows * MOST_BLK * block * columns,
            bytes_accessed=4 * rows * columns + 2 * span * own.shape[1],
            transcendentals=rows * MOST_BLK * block * heads,
        ),
        name="attend",
    )(first, count, query, before, own, after)


def on_device(tokens, norm_gain, w_query, w_key, w_value, passage_blocks):
    groups, peers = lax.axis_size("groups"), lax.axis_size("seq")
    team = w_key.shape[1] // HD
    depth = w_key.shape[0]
    rows = tokens.shape[0]
    blocks = passage_blocks.shape[0]
    block = rows // blocks
    index = lax.axis_index("seq")
    group, layer, member = lax.axis_index("groups"), index // team, index % team
    place = jnp.stack([group, layer, member]).astype(jnp.int32)
    q_columns = w_query.shape[1] // team

    def columns_of(weight, r):
        width = weight.shape[1] // team
        return lax.dynamic_slice_in_dim(weight, (member ^ r) * width, width, 1)

    kv_blocks = [
        jnp.concatenate([columns_of(w_key, r), columns_of(w_value, r)], axis=1)
        for r in range(team)
    ]
    q_blocks = [columns_of(w_query, r) for r in range(team)]

    normed = normalize(tokens, norm_gain)
    near = swap(normed, team, 0, 0, 1)
    far = [swap(normed, team, 0, 0, 2)]
    far.append(swap(far[0], team, 0, 0, 1))
    team_tokens = [normed, near] + far

    if depth // groups % LANES == 0:
        kv_found = gather_columns(kv_blocks, team, place)
        q_found = gather_columns(q_blocks, team, place)
        keys_values = project(place, team_tokens, kv_found, groups, depth)
        query = project(place, team_tokens, q_found, groups, depth)
    else:
        in_order = [None] * team
        stacked = jnp.stack(team_tokens)
        in_order = jnp.concatenate(
            [lax.dynamic_index_in_dim(stacked, member ^ t, 0, False) for t in range(team)]
        )

        def whole(weight):
            full = lax.all_gather(weight, "seq", axis=0, tiled=True)
            return columns_of(full, 0)

        def dense(weight):
            product = jnp.dot(in_order, weight, preferred_element_type=jnp.float32)
            return product.astype(jnp.bfloat16)

        keys_values = jnp.concatenate([dense(whole(w_key)), dense(whole(w_value))], axis=1)
        query = dense(whole(w_query))

    margin = (MOST_BLK - 1) * block
    before = from_layer(keys_values[-margin:], team, -1)
    after = from_layer(keys_values[:margin], team, 1)

    ids = lax.all_gather(passage_blocks, "seq", axis=0, tiled=True)
    mine = lax.dynamic_slice_in_dim(ids, layer * team * blocks, team * blocks, 0)
    same = mine[:, None] == ids[None, :]
    count = jnp.sum(same.astype(jnp.int32), axis=1)
    first = jnp.sum((ids[None, :] < mine[:, None]).astype(jnp.int32), axis=1)
    first = first - layer * team * blocks + (MOST_BLK - 1)

    attended = attend(first, count, query, before, keys_values, after, block)

    def rows_of(r):
        return lax.dynamic_slice_in_dim(attended, (member ^ r) * rows, rows, 0)

    out = jnp.zeros((rows, w_query.shape[1]), jnp.bfloat16)
    for r in range(team):
        piece = rows_of(r)
        if r:
            piece = swap(piece, team, 0, 0, r)
        out = lax.dynamic_update_slice(out, piece, (0, (member ^ r) * q_columns))
    return out


def solution(mesh):
    in_specs = (
        P(("groups", "seq"), None),
        P(),
        P("seq", None),
        P("seq", None),
        P("seq", None),
        P(("groups", "seq")),
    )
    out_specs = P(("groups", "seq"), None)
    return jax.shard_map(
        on_device, mesh=mesh, in_specs=in_specs, out_specs=out_specs, check_vma=False
    )
```

```python
import functools

import jax
import jax.numpy as jnp
from jax import lax
from jax.experimental import pallas as pl
from jax.experimental.pallas import tpu as pltpu
from jax.sharding import PartitionSpec as P

HD = 128
MOST_BLK = 7
LANES = 128
NOTES = 16
AXES = ("groups", "seq")
LOG2_E = 1.4426950408889634
VMEM_LIMIT = 63 * 1024 * 1024
IN_VMEM = pl.BlockSpec(memory_space=pltpu.VMEM)
IN_SMEM = pl.BlockSpec(memory_space=pltpu.SMEM)
IN_HBM = pl.BlockSpec(memory_space=pltpu.HBM)
PARAMS = pltpu.CompilerParams(vmem_limit_bytes=VMEM_LIMIT)


def cost(flops, size, transcendentals=0):
    return pl.CostEstimate(
        flops=flops, bytes_accessed=size, transcendentals=transcendentals
    )


def swap(value, team, group_bits, layer_bits, member_bits):
    groups, peers = lax.axis_size("groups"), lax.axis_size("seq")
    pairs = []
    for g in range(groups):
        for s in range(peers):
            layer, member = divmod(s, team)
            to = (layer ^ layer_bits) * team + (member ^ member_bits)
            pairs.append((g * peers + s, (g ^ group_bits) * peers + to))
    return lax.ppermute(value, AXES, pairs)


def from_layer(value, team, by):
    groups, peers = lax.axis_size("groups"), lax.axis_size("seq")
    pairs = []
    for g in range(groups):
        for s in range(peers):
            to = s - by * team
            if 0 <= to < peers:
                pairs.append((g * peers + s, g * peers + to))
    return lax.ppermute(value, AXES, pairs)


def tie(value, *others):
    return lax.optimization_barrier((value,) + others)[0] if others else value


def norm_kernel(tokens_ref, gain_ref, *outs):
    first = 0
    for out in outs:
        widened = tokens_ref[first : first + out.shape[0], :].astype(jnp.float32)
        square = jnp.mean(widened * widened, axis=-1, keepdims=True)
        out[...] = (widened * lax.rsqrt(square + 1e-05) * gain_ref[...]).astype(jnp.bfloat16)
        first += out.shape[0]


def normalize(tokens, norm_gain, lengths):
    rows, width = tokens.shape
    return pl.pallas_call(
        norm_kernel,
        out_shape=[jax.ShapeDtypeStruct((n, width), jnp.bfloat16) for n in lengths],
        in_specs=[IN_VMEM] * 2,
        out_specs=[IN_VMEM] * len(lengths),
        compiler_params=PARAMS,
        cost_estimate=cost(6 * rows * width, 4 * rows * width, rows),
        name="normalize",
    )(tokens, norm_gain.reshape(1, width))


def pack_kernel(team, part, count, place, numbers, *refs):
    weights, outs = refs[:count], refs[count : count + team]
    loaded, sems = refs[count + team : -1], refs[-1]
    copies = [
        pltpu.make_async_copy(weight, there, sems.at[i])
        for i, (weight, there) in enumerate(zip(weights, loaded))
    ]
    for copy in copies:
        copy.start()
    row = lax.broadcasted_iota(jnp.int32, (NOTES, outs[0].shape[1]), 0)
    noted = jnp.zeros((NOTES, outs[0].shape[1]), jnp.float32)
    for i in range(numbers.shape[0]):
        noted = jnp.where(row == i, numbers[i].astype(jnp.float32), noted)
    noted = noted.astype(jnp.bfloat16)
    for out in outs:
        out[out.shape[0] - NOTES :, :] = noted
    column = 0
    for copy, weight in zip(copies, loaded):
        copy.wait()
        width = weight.shape[1] // team
        for r, out in enumerate(outs):
            length = out.shape[0] - NOTES
            first = 0 if r < 2 else pl.multiple_of(place[0] * part, part)
            columns = pl.ds(pl.multiple_of((place[2] ^ r) * width, width), width)
            out[:length, column : column + width] = weight[pl.ds(first, length), columns]
        column += width


def pack(place, numbers, weights, team, groups):
    depth = weights[0].shape[0]
    width = sum(weight.shape[1] for weight in weights) // team
    lengths = [depth if r < 2 else depth // groups for r in range(team)]
    return pl.pallas_call(
        functools.partial(pack_kernel, team, depth // groups, len(weights)),
        out_shape=[
            jax.ShapeDtypeStruct((length + NOTES, width), jnp.bfloat16)
            for length in lengths
        ],
        in_specs=[IN_SMEM] * 2 + [IN_HBM] * len(weights),
        out_specs=[IN_VMEM] * team,
        scratch_shapes=[pltpu.VMEM(w.shape, w.dtype) for w in weights]
        + [pltpu.SemaphoreType.DMA((len(weights),))],
        compiler_params=PARAMS,
        cost_estimate=cost(0, 4 * team * depth * width),
        name="pack",
    )(place, numbers, *weights)


def shards_kernel(team, part, blocks, place, *refs):
    ins, shards, far = refs[:team], refs[team:-1], refs[-1]
    mine = pl.ds(pl.multiple_of(place[0] * part, part), part)
    for r, ref in enumerate(ins):
        rows = mine if r < 2 else pl.ds(0, part)
        column = 0
        for shard in shards:
            width = shard.shape[1]
            shard[r * part : (r + 1) * part, :] = ref[rows, column : column + width]
            column += width
        if r >= 2:
            far[(r - 2) * part : (r - 1) * part, :] = ref[rows, :]
    noted_in = shards[0]
    row = lax.broadcasted_iota(jnp.int32, (NOTES, noted_in.shape[1]), 0)
    noted = jnp.zeros((NOTES, noted_in.shape[1]), jnp.float32)
    for r, ref in enumerate(ins):
        held = ref[ref.shape[0] - NOTES :, : noted_in.shape[1]].astype(jnp.float32)
        for i in range(blocks):
            noted = jnp.where(row == r * blocks + i, held[i : i + 1, :], noted)
    noted_in[team * part :, :] = noted.astype(jnp.bfloat16)


def make_shards(place, packed, moved, widths, depth, groups, blocks):
    part, width = depth // groups, packed.shape[1]
    team = 1 + len(moved)
    shapes = [(team * part + (0 if i else NOTES), w) for i, w in enumerate(widths)]
    shapes.append(((team - 2) * part, width))
    return pl.pallas_call(
        functools.partial(shards_kernel, team, part, blocks),
        out_shape=[jax.ShapeDtypeStruct(shape, jnp.bfloat16) for shape in shapes],
        in_specs=[IN_SMEM] + [IN_VMEM] * team,
        out_specs=[IN_VMEM] * len(shapes),
        compiler_params=PARAMS,
        cost_estimate=cost(0, 6 * team * part * width),
        name="shards",
    )(place, packed, *moved)


def project_kernel(items, counts, chunk, margin, rest, team, groups, depth, place, *refs):
    held, arrays, wanted = counts
    sources, refs = refs[:held], refs[held:]
    stored, refs = refs[:arrays], refs[arrays:]
    outs, (tokens, weights, total, token_sems, sems) = refs[:-5], refs[-5:]
    part = depth // groups
    group, layer, member = place[0], place[1], place[2]
    span = tokens.shape[0] // 2
    token_copies, offset = ([], []), 0
    for i, ref in enumerate(sources):
        there = tokens.at[pl.ds(offset, ref.shape[0])]
        copy = pltpu.make_async_copy(ref, there, token_sems.at[i])
        token_copies[offset // span].append(copy)
        offset += ref.shape[0]
    for copy in token_copies[0]:
        copy.start()
    plan, offset, copies = [], 0, 0
    for described, parts in items:
        deep = sum(depth if bits[2] is None else part for bits in described)
        loads = []
        for c, (source, first, column) in enumerate(parts):
            copy = pltpu.make_async_copy(
                stored[source].at[pl.ds(first, deep), pl.ds(column, chunk)],
                weights.at[pl.ds(offset, deep), pl.ds(c * chunk, chunk)],
                sems.at[copies],
            )
            copy.start()
            loads.append(copy)
            copies += 1
        plan.append((described, offset, deep, loads))
        offset += deep

    def columns_of(own, described):
        lefts = []
        for layer_bits, member_bits, group_bits in described:
            owner = (layer ^ layer_bits) * team + (member ^ member_bits)
            first, wide = owner * depth, depth
            if group_bits is not None:
                first, wide = first + (group ^ group_bits) * part, part
            lefts.append(tokens[own, pl.ds(pl.multiple_of(first, LANES), wide)])
        return lefts[0] if len(lefts) == 1 else jnp.concatenate(lefts, axis=1)

    for half in range(2):
        own = pl.ds(half * span, span)
        for copy in token_copies[half]:
            copy.wait()
        if half == 0:
            for copy in token_copies[1]:
                copy.start()
        for i, (described, offset, deep, loads) in enumerate(plan):
            if half == 0:
                for copy in loads:
                    copy.wait()
            wide = len(loads) * chunk
            right = weights[pl.ds(offset, deep), :wide]
            term = jnp.dot(
                columns_of(own, described), right, preferred_element_type=jnp.float32
            )
            if i == 0:
                total[own, :wide] = term
            else:
                total[own, :wide] += term
        column = 0
        for described in rest if wanted else ():
            left = columns_of(own, described)
            outs[-1][own, column : column + left.shape[1]] = left
            column += left.shape[1]
    rows = total.shape[0] // team
    chunks = total.shape[1] // chunk
    for c in range(chunks):
        columns = slice(c * chunk, (c + 1) * chunk)
        if rest and c + 1 == chunks:
            outs[c][...] = total[:, columns]
            continue
        for r in range(team):
            first = r * rows
            if c == 0 and margin is not None:
                first = pl.multiple_of((member ^ r) * rows, rows)
            made = total[r * rows : (r + 1) * rows, columns]
            outs[c][pl.ds(first, rows), :] = made.astype(jnp.bfloat16)
    if margin is not None:
        outs[chunks][...] = outs[0][total.shape[0] - margin :, :]
        outs[chunks + 1][...] = outs[0][:margin, :]


def project(
    place, team, tokens, arrays, items, chunk, groups, depth, margin=None, rest=(), wanted=False
):
    count, width = sum(value.shape[0] for value in tokens), tokens[0].shape[1]
    chunks = max(len(parts) for _, parts in items)
    names = sorted({name for _, parts in items for name, _, _ in parts})
    items = [
        (described, [(names.index(n), first, column) for n, first, column in parts])
        for described, parts in items
        if parts
    ]

    def deep_of(listed):
        return sum(depth // (1 if b[2] is None else groups) for d in listed for b in d)

    deep = deep_of([described for described, _ in items])
    copies = sum(len(parts) for _, parts in items)
    kinds = [jnp.bfloat16] * (chunks - bool(rest)) + [jnp.float32] * bool(rest)
    shapes = [jax.ShapeDtypeStruct((count, chunk), kind) for kind in kinds]
    if margin is not None:
        shapes += [jax.ShapeDtypeStruct((margin, chunk), jnp.bfloat16)] * 2
    if wanted:
        shapes.append(jax.ShapeDtypeStruct((count, deep_of(rest)), jnp.bfloat16))
    return pl.pallas_call(
        functools.partial(
            project_kernel,
            items,
            (len(tokens), len(names), wanted),
            chunk,
            margin,
            rest,
            team,
            groups,
            depth,
        ),
        out_shape=shapes,
        in_specs=[IN_SMEM] + [IN_HBM] * (len(tokens) + len(names)),
        out_specs=[IN_VMEM] * len(shapes),
        scratch_shapes=[
            pltpu.VMEM((count, width), jnp.bfloat16),
            pltpu.VMEM((deep, chunks * chunk), jnp.bfloat16),
            pltpu.VMEM((count, chunks * chunk), jnp.float32),
            pltpu.SemaphoreType.DMA((len(tokens),)),
            pltpu.SemaphoreType.DMA((copies,)),
        ],
        compiler_params=PARAMS,
        cost_estimate=cost(
            2 * count * deep * chunks * chunk,
            2 * chunks * chunk * (count + deep) + 2 * count * width,
        ),
        name="project",
    )(place, *tokens, *[arrays[name] for name in names])


def attend_kernel(
    base, block, deep, firsts, first_ref, count_ref, before, own, after, *refs
):
    outs, (window, query) = refs[:-2][-(len(refs) - 2 - firsts[0]) :], refs[-2:]
    ins = refs[: firsts[0]]
    per_out = outs[0].shape[0] // block
    total_blocks = per_out * len(outs)
    mine = pl.ds(base * block, total_blocks * block)
    if deep:
        *sums, left = ins[: len(firsts[1]) + 1]
        weights = iter(ins[len(firsts[1]) + 1 :])
        for c, (begun, starts) in enumerate(zip(sums, firsts[1])):
            total = begun[mine, :]
            for i, start in enumerate(starts):
                total += jnp.dot(
                    left[mine, i * deep : (i + 1) * deep],
                    next(weights)[start : start + deep, :],
                    preferred_element_type=jnp.float32,
                )
            wide = total.shape[1]
            query[:, c * wide : (c + 1) * wide] = total.astype(jnp.bfloat16)
    else:
        query[...] = ins[0][mine, :]
    offset = 0
    for ref in (before, own, after):
        window[offset : offset + ref.shape[0], :] = ref[...]
        offset += ref.shape[0]
    heads = query.shape[1] // HD
    span = MOST_BLK * block
    row = lax.broadcasted_iota(jnp.int32, (span, 1), 0)

    def place_of(b):
        return pl.ds(pl.multiple_of(first_ref[base + b] * block, block), span)

    def score(b):
        rows = pl.ds(b * block, block)
        stacked = jnp.concatenate(
            [query[rows, h * HD : (h + 1) * HD] for h in range(heads)], axis=0
        )
        return lax.dot_general(
            window[place_of(b), :HD],
            stacked,
            (((1,), (1,)), ((), ())),
            preferred_element_type=jnp.float32,
        )

    scores = score(0)
    for b in range(total_blocks):
        upcoming = score(b + 1) if b + 1 < total_blocks else None
        scores = jnp.where(row < count_ref[base + b] * block, scores, -1e30)
        row_max = jnp.max(scores, axis=0, keepdims=True)
        weights = jnp.exp2((scores - row_max) * (HD ** (-0.5) * LOG2_E))
        row_total = jnp.sum(weights, axis=0, keepdims=True)
        mixed = lax.dot_general(
            window[place_of(b), HD:],
            weights.astype(jnp.bfloat16),
            (((0,), (0,)), ((), ())),
            preferred_element_type=jnp.float32,
        )
        mixed = mixed / row_total
        out = outs[b // per_out]
        rows = pl.ds((b % per_out) * block, block)
        for h in range(heads):
            turned = mixed[:, h * block : (h + 1) * block].T
            out[rows, h * HD : (h + 1) * HD] = turned.astype(jnp.bfloat16)
        scores = upcoming


def attend(first, count, query, before, own, after, block, base, rows, parts):
    if isinstance(query, tuple):
        *sums, left, lates = query
        ins = [*sums, left] + [array for late in lates for array, _ in late]
        firsts = (len(ins), [[start for _, start in late] for late in lates])
        deep = left.shape[1] // len(lates[0])
        columns = sum(value.shape[1] for value in sums)
    else:
        ins, firsts, deep, columns = [query], (1, []), 0, query.shape[1]
    span = before.shape[0] + own.shape[0] + after.shape[0]
    return pl.pallas_call(
        functools.partial(attend_kernel, base, block, deep, firsts),
        out_shape=[jax.ShapeDtypeStruct((rows, columns), jnp.bfloat16)] * parts,
        in_specs=[IN_SMEM] * 2 + [IN_VMEM] * (3 + len(ins)),
        out_specs=[IN_VMEM] * parts,
        scratch_shapes=[
            pltpu.VMEM((span, own.shape[1]), jnp.bfloat16),
            pltpu.VMEM((parts * rows, columns), jnp.bfloat16),
        ],
        compiler_params=PARAMS,
        cost_estimate=cost(
            4 * parts * rows * MOST_BLK * block * columns,
            4 * rows * columns + 2 * span * own.shape[1],
            parts * rows * MOST_BLK * block * (columns // HD),
        ),
        name="attend",
    )(first, count, before, own, after, *ins)


def assemble_kernel(place, *refs):
    pieces, out = refs[:-1], refs[-1]
    for r, piece in enumerate(pieces):
        width = piece.shape[1]
        first = pl.multiple_of((place[2] ^ r) * width, width)
        out[:, pl.ds(first, width)] = piece[...]


def assemble(place, pieces):
    rows, width = pieces[0].shape
    return pl.pallas_call(
        assemble_kernel,
        out_shape=jax.ShapeDtypeStruct((rows, width * len(pieces)), jnp.bfloat16),
        in_specs=[IN_SMEM] + [IN_VMEM] * len(pieces),
        out_specs=IN_VMEM,
        compiler_params=PARAMS,
        cost_estimate=cost(0, 4 * rows * width * len(pieces)),
        name="assemble",
    )(place, *pieces)


def on_device(tokens, norm_gain, w_query, w_key, w_value, passage_blocks):
    groups, peers = lax.axis_size("groups"), lax.axis_size("seq")
    team = w_key.shape[1] // HD
    layers = peers // team
    depth = w_key.shape[0]
    rows = tokens.shape[0]
    blocks = passage_blocks.shape[0]
    block = rows // blocks
    index = lax.axis_index("seq")
    group, layer, member = lax.axis_index("groups"), index // team, index % team
    place = jnp.stack([group, layer, member]).astype(jnp.int32)
    widths = [2 * HD] * ((w_key.shape[1] + w_value.shape[1] + w_query.shape[1]) // (2 * HD * team))
    margin = (MOST_BLK - 1) * block

    if depth // groups % LANES == 0 and team * blocks <= NOTES:
        chunk = 2 * HD
        packed = pack(place, passage_blocks, [w_key, w_value, w_query], team, groups)
        moved = [swap(packed[r], team, 0, 0, r) for r in range(1, team)]
        steps = range(1, 4)
        lengths = [rows * n // 16 for n in (4, 6, 6)]
        normed = normalize(tie(tokens, packed[0]), norm_gain, lengths)
        *shards, far = make_shards(
            tie(place, normed[0]), packed[0], moved, widths, depth, groups, blocks
        )

        chunks = len(shards)
        hops = max(bits.bit_count() for bits in range(layers))
        arrays = {"own": packed[0], "far": far}
        arrays.update({f"normed{i}": value for i, value in zip(steps, normed)})
        arrays.update({f"moved{r}": value for r, value in enumerate(moved, 1)})
        arrays.update({f"shard{c}": shard for c, shard in enumerate(shards)})
        held = {(c, 0): (f"shard{c}", 0, shard.shape[0]) for c, shard in enumerate(shards)}
        crossed, far_tokens, diagonal = {}, [], []
        part = depth // groups

        def join(parts):
            views = [arrays[name][first : first + n] for name, first, n in parts]
            return views[0] if len(views) == 1 else jnp.concatenate(views, axis=0)

        def items_of(cs, layer_bits=range(layers), others=range(groups)):
            items = []
            if 0 in layer_bits:
                for r, name in enumerate(["own"] + [f"moved{r}" for r in range(1, team)]):
                    described = [(0, r, None if r < 2 else 0)]
                    items.append((described, [(name, 0, c * chunk) for c in cs]))
                for other in range(1, groups):
                    described = [(0, r, other) for r in range(2, team)]
                    items.append((described, [(f"far{other}", 0, c * chunk) for c in cs]))
            for other in others:
                for bits in layer_bits:
                    if bits:
                        described = [(bits, r, other) for r in range(team)]
                        where = [crossed[c, bits, other] if other else held[c, bits] for c in cs]
                        items.append((described, [(n, first, 0) for n, first, _ in where]))
            return items

        hardest = [bits for bits in range(layers) if bits.bit_count() == hops]

        def without_last(cs):
            items, rest, late = [], [], []
            for described, parts in items_of(cs):
                if described[0][2] and described[0][0] in hardest:
                    name, first, _ = parts[-1]
                    late.append((name, first))
                    rest.append(described)
                    parts = parts[:-1]
                items.append((described, parts))
            late = [(arrays[n], f) for n, f in late if n in arrays]
            return items, rest, late

        for phase in range(1, chunks + hops + 1):
            arrays = lax.optimization_barrier(arrays)
            sends = []
            ways = {}
            for c in range(chunks):
                for bits in range(1, layers):
                    low = bits & -bits
                    if c + bits.bit_count() == phase:
                        ways.setdefault((0, low), []).append((c, bits, held[c, bits ^ low]))
                    elif c + bits.bit_count() + 1 == phase:
                        for other in range(1, groups):
                            way = ways.setdefault((other, 0), [])
                            way.append((c, bits, held[c, bits]))
            for (other, low), listed in ways.items():
                name = f"phase{phase}from{other}{low}"
                value = join([p for _, _, p in listed])
                sends.append((other, low, 0, name, value))
                first = 0
                for c, bits, (_, _, n) in listed:
                    if other:
                        crossed[c, bits, other] = (name, first, n)
                    else:
                        held[c, bits] = (name, first, n)
                    first += n
            if phase in steps:
                sends.append((0, 0, 2, f"tokens{phase}", arrays[f"normed{phase}"]))
            if phase - 1 in steps:
                value = arrays[f"tokens{phase - 1}"]
                sends.append((0, 0, 1, f"diagonal{phase - 1}", value))
            if phase == 1:
                for i in steps:
                    sends.append((0, 0, 1, f"near{i}", arrays[f"normed{i}"]))
                for other in range(1, groups):
                    sends.append((other, 0, 0, f"far{other}", arrays["far"]))
            new = {}
            for group_bits, layer_bits, member_bits, name, value in sends:
                new[name] = swap(value, team, group_bits, layer_bits, member_bits)
            arrays.update(new)
            if phase == chunks + hops - 1:
                team_tokens = [arrays[f"normed{i}"] for i in steps]
                team_tokens += [arrays[f"near{i}"] for i in steps]
                team_tokens += [arrays[f"tokens{i}"] for i in steps]
                team_tokens += [arrays[f"diagonal{i}"] for i in steps]
                items, rest, _ = without_last(range(chunks - 1))
                made = project(
                    place,
                    team,
                    team_tokens,
                    arrays,
                    items,
                    chunk,
                    groups,
                    depth,
                    margin,
                    rest,
                    True,
                )
                names = ["keys_values"] + [f"sum{c}" for c in range(1, chunks - 1)]
                arrays.update(zip(names + ["tail", "head", "left"], made))
        team_tokens = [arrays[f"normed{i}"] for i in steps]
        team_tokens += [arrays[f"near{i}"] for i in steps]
        team_tokens += [arrays[f"tokens{i}"] for i in steps]
        team_tokens += [arrays[f"diagonal{i}"] for i in steps]
        keys_values, tail, head = (arrays[n] for n in ("keys_values", "tail", "head"))
        items, rest, late = without_last([chunks - 1])
        (begun,) = project(
            place, team, team_tokens, arrays, items, chunk, groups, depth, rest=rest
        )
        lates = [without_last([chunks - 2])[2], late]
        query = (arrays[f"sum{chunks - 2}"], begun, arrays["left"], lates)
        assert chunks == 3
        ids = []
        for s in range(layers):
            name, first, n = held[0, s]
            noted = arrays[name][first + team * part : first + n]
            ids.append(noted[: team * blocks, 0])
        ids = jnp.stack(ids).astype(jnp.int32)
        mine = ids[0]
        ids = ids.reshape(-1)
    else:
        (normed,) = normalize(tokens, norm_gain, [rows])
        team_tokens = [normed] + [swap(normed, team, 0, 0, r) for r in range(1, team)]
        stacked = jnp.stack(team_tokens)
        in_order = jnp.concatenate(
            [lax.dynamic_index_in_dim(stacked, member ^ t, 0, False) for t in range(team)]
        )

        def dense(weight, rows_of_tokens):
            whole = lax.all_gather(weight, "seq", axis=0, tiled=True)
            width = weight.shape[1] // team
            own = lax.dynamic_slice_in_dim(whole, member * width, width, 1)
            product = jnp.dot(rows_of_tokens, own, preferred_element_type=jnp.float32)
            return product.astype(jnp.bfloat16)

        keys_values = jnp.concatenate(
            [dense(w_key, in_order), dense(w_value, in_order)], axis=1
        )
        tail, head = keys_values[-margin:], keys_values[:margin]
        query = dense(w_query, stacked.reshape(team * rows, tokens.shape[1]))
        ids = lax.all_gather(passage_blocks, "seq", axis=0, tiled=True)
        mine = jnp.concatenate(
            [
                lax.dynamic_slice_in_dim(ids, (layer * team + (member ^ r)) * blocks, blocks)
                for r in range(team)
            ]
        )

    before = from_layer(tail, team, -1)
    after = from_layer(head, team, 1)

    count = jnp.sum((mine[:, None] == ids[None, :]).astype(jnp.int32), axis=1)
    first = jnp.sum((ids[None, :] < mine[:, None]).astype(jnp.int32), axis=1)
    first = first - layer * team * blocks + (MOST_BLK - 1)

    pieces = [None] * team
    for start, end in ((1, team), (0, 1)):
        made = attend(
            first,
            count,
            query,
            before,
            keys_values,
            after,
            block,
            start * blocks,
            rows,
            end - start,
        )
        for r, piece in enumerate(made, start):
            pieces[r] = swap(piece, team, 0, 0, r) if r else piece
    return assemble(place, pieces)


def solution(mesh):
    in_specs = (
        P(("groups", "seq"), None),
        P(),
        P("seq", None),
        P("seq", None),
        P("seq", None),
        P(("groups", "seq")),
    )
    out_specs = P(("groups", "seq"), None)
    return jax.shard_map(
        on_device, mesh=mesh, in_specs=in_specs, out_specs=out_specs, check_vma=False
    )
```

```python
import functools

import jax
import jax.numpy as jnp
from jax import lax
from jax.experimental import pallas as pl
from jax.experimental.pallas import tpu as pltpu
from jax.sharding import PartitionSpec as P

HD = 128
MOST_BLK = 7
LANES = 128
NOTES = 16
AXES = ("groups", "seq")
LOG2_E = 1.4426950408889634
VMEM_LIMIT = 63 * 1024 * 1024
IN_VMEM = pl.BlockSpec(memory_space=pltpu.VMEM)
IN_SMEM = pl.BlockSpec(memory_space=pltpu.SMEM)
IN_HBM = pl.BlockSpec(memory_space=pltpu.HBM)
PARAMS = pltpu.CompilerParams(vmem_limit_bytes=VMEM_LIMIT)


def cost(flops, size, transcendentals=0):
    return pl.CostEstimate(
        flops=flops, bytes_accessed=size, transcendentals=transcendentals
    )


def swap(value, team, group_bits, layer_bits, member_bits):
    groups, peers = lax.axis_size("groups"), lax.axis_size("seq")
    pairs = []
    for g in range(groups):
        for s in range(peers):
            layer, member = divmod(s, team)
            to = (layer ^ layer_bits) * team + (member ^ member_bits)
            pairs.append((g * peers + s, (g ^ group_bits) * peers + to))
    return lax.ppermute(value, AXES, pairs)


def from_layer(value, team, by):
    groups, peers = lax.axis_size("groups"), lax.axis_size("seq")
    pairs = []
    for g in range(groups):
        for s in range(peers):
            to = s - by * team
            if 0 <= to < peers:
                pairs.append((g * peers + s, g * peers + to))
    return lax.ppermute(value, AXES, pairs)


def tie(value, *others):
    return lax.optimization_barrier((value,) + others)[0] if others else value


def norm_kernel(tokens_ref, gain_ref, *outs):
    first = 0
    for out in outs:
        widened = tokens_ref[first : first + out.shape[0], :].astype(jnp.float32)
        square = jnp.mean(widened * widened, axis=-1, keepdims=True)
        out[...] = (widened * lax.rsqrt(square + 1e-05) * gain_ref[...]).astype(jnp.bfloat16)
        first += out.shape[0]


def normalize(tokens, norm_gain, lengths):
    rows, width = tokens.shape
    return pl.pallas_call(
        norm_kernel,
        out_shape=[jax.ShapeDtypeStruct((n, width), jnp.bfloat16) for n in lengths],
        in_specs=[IN_VMEM] * 2,
        out_specs=[IN_VMEM] * len(lengths),
        compiler_params=PARAMS,
        cost_estimate=cost(6 * rows * width, 4 * rows * width, rows),
        name="normalize",
    )(tokens, norm_gain.reshape(1, width))


def pack_kernel(team, part, count, place, numbers, *refs):
    weights, outs = refs[:count], refs[count : count + team]
    loaded, sems = refs[count + team : -1], refs[-1]
    copies = [
        pltpu.make_async_copy(weight, there, sems.at[i])
        for i, (weight, there) in enumerate(zip(weights, loaded))
    ]
    for copy in copies:
        copy.start()
    row = lax.broadcasted_iota(jnp.int32, (NOTES, outs[0].shape[1]), 0)
    noted = jnp.zeros((NOTES, outs[0].shape[1]), jnp.float32)
    for i in range(numbers.shape[0]):
        noted = jnp.where(row == i, numbers[i].astype(jnp.float32), noted)
    noted = noted.astype(jnp.bfloat16)
    for out in outs:
        out[out.shape[0] - NOTES :, :] = noted
    column = 0
    for copy, weight in zip(copies, loaded):
        copy.wait()
        width = weight.shape[1] // team
        for r, out in enumerate(outs):
            length = out.shape[0] - NOTES
            first = 0 if r < 2 else pl.multiple_of(place[0] * part, part)
            columns = pl.ds(pl.multiple_of((place[2] ^ r) * width, width), width)
            out[:length, column : column + width] = weight[pl.ds(first, length), columns]
        column += width


def pack(place, numbers, weights, team, groups):
    depth = weights[0].shape[0]
    width = sum(weight.shape[1] for weight in weights) // team
    lengths = [depth if r < 2 else depth // groups for r in range(team)]
    return pl.pallas_call(
        functools.partial(pack_kernel, team, depth // groups, len(weights)),
        out_shape=[
            jax.ShapeDtypeStruct((length + NOTES, width), jnp.bfloat16)
            for length in lengths
        ],
        in_specs=[IN_SMEM] * 2 + [IN_HBM] * len(weights),
        out_specs=[IN_VMEM] * team,
        scratch_shapes=[pltpu.VMEM(w.shape, w.dtype) for w in weights]
        + [pltpu.SemaphoreType.DMA((len(weights),))],
        compiler_params=PARAMS,
        cost_estimate=cost(0, 4 * team * depth * width),
        name="pack",
    )(place, numbers, *weights)


def shards_kernel(team, part, blocks, place, *refs):
    ins, shards, far = refs[:team], refs[team:-1], refs[-1]
    mine = pl.ds(pl.multiple_of(place[0] * part, part), part)
    for r, ref in enumerate(ins):
        rows = mine if r < 2 else pl.ds(0, part)
        column = 0
        for shard in shards:
            width = shard.shape[1]
            shard[r * part : (r + 1) * part, :] = ref[rows, column : column + width]
            column += width
        if r >= 2:
            far[(r - 2) * part : (r - 1) * part, :] = ref[rows, :]
    noted_in = shards[0]
    row = lax.broadcasted_iota(jnp.int32, (NOTES, noted_in.shape[1]), 0)
    noted = jnp.zeros((NOTES, noted_in.shape[1]), jnp.float32)
    for r, ref in enumerate(ins):
        held = ref[ref.shape[0] - NOTES :, : noted_in.shape[1]].astype(jnp.float32)
        for i in range(blocks):
            noted = jnp.where(row == r * blocks + i, held[i : i + 1, :], noted)
    noted_in[team * part :, :] = noted.astype(jnp.bfloat16)


def make_shards(place, packed, moved, widths, depth, groups, blocks):
    part, width = depth // groups, packed.shape[1]
    team = 1 + len(moved)
    shapes = [(team * part + (0 if i else NOTES), w) for i, w in enumerate(widths)]
    shapes.append(((team - 2) * part, width))
    return pl.pallas_call(
        functools.partial(shards_kernel, team, part, blocks),
        out_shape=[jax.ShapeDtypeStruct(shape, jnp.bfloat16) for shape in shapes],
        in_specs=[IN_SMEM] + [IN_VMEM] * team,
        out_specs=[IN_VMEM] * len(shapes),
        compiler_params=PARAMS,
        cost_estimate=cost(0, 6 * team * part * width),
        name="shards",
    )(place, packed, *moved)


def project_kernel(items, counts, chunk, margin, rest, team, groups, depth, place, *refs):
    held, arrays, wanted = counts
    sources, refs = refs[:held], refs[held:]
    stored, refs = refs[:arrays], refs[arrays:]
    outs, (tokens, weights, total, token_sems, sems) = refs[:-5], refs[-5:]
    part = depth // groups
    group, layer, member = place[0], place[1], place[2]
    layer_wide = team * depth
    layers = sorted({described[0][0] for described, _ in items})
    plan, offset, copies, token_copies = [], 0, 0, 0
    for layer_bits in layers:
        loads, matched, row = [], [], 0
        first = pl.multiple_of((layer ^ layer_bits) * layer_wide, LANES)
        for ref in sources:
            here = pl.ds(first, layer_wide)
            there = tokens.at[pl.ds(row, ref.shape[0]), here]
            loads.append(
                pltpu.make_async_copy(ref.at[:, here], there, token_sems.at[token_copies])
            )
            row += ref.shape[0]
            token_copies += 1
        for described, parts in items:
            if described[0][0] != layer_bits:
                continue
            deep = sum(depth if bits[2] is None else part for bits in described)
            for c, (source, first, column) in enumerate(parts):
                loads.append(
                    pltpu.make_async_copy(
                        stored[source].at[pl.ds(first, deep), pl.ds(column, chunk)],
                        weights.at[pl.ds(offset, deep), pl.ds(c * chunk, chunk)],
                        sems.at[copies],
                    )
                )
                copies += 1
            matched.append((described, offset, deep, len(parts) * chunk))
            offset += deep
        for copy in loads:
            copy.start()
        plan.append((loads, matched))

    def columns_of(own, described):
        lefts = []
        for layer_bits, member_bits, group_bits in described:
            owner = (layer ^ layer_bits) * team + (member ^ member_bits)
            first, wide = owner * depth, depth
            if group_bits is not None:
                first, wide = first + (group ^ group_bits) * part, part
            lefts.append(tokens[own, pl.ds(pl.multiple_of(first, LANES), wide)])
        return lefts[0] if len(lefts) == 1 else jnp.concatenate(lefts, axis=1)

    span = tokens.shape[0] // 2
    for step, (loads, matched) in enumerate(plan):
        for copy in loads:
            copy.wait()
        for half in range(2):
            own = pl.ds(half * span, span)
            for i, (described, offset, deep, wide) in enumerate(matched):
                right = weights[pl.ds(offset, deep), :wide]
                term = jnp.dot(
                    columns_of(own, described), right, preferred_element_type=jnp.float32
                )
                if i == 0 and step == 0:
                    total[own, :wide] = term
                else:
                    total[own, :wide] += term
    if wanted:
        column = 0
        for described in rest:
            left = columns_of(pl.ds(0, tokens.shape[0]), described)
            outs[-1][:, column : column + left.shape[1]] = left
            column += left.shape[1]
    rows = total.shape[0] // team
    chunks = total.shape[1] // chunk
    for c in range(chunks):
        columns = slice(c * chunk, (c + 1) * chunk)
        if rest and c + 1 == chunks:
            outs[c][...] = total[:, columns]
            continue
        for r in range(team):
            first = r * rows
            if c == 0 and margin is not None:
                first = pl.multiple_of((member ^ r) * rows, rows)
            made = total[r * rows : (r + 1) * rows, columns]
            outs[c][pl.ds(first, rows), :] = made.astype(jnp.bfloat16)
    if margin is not None:
        outs[chunks][...] = outs[0][total.shape[0] - margin :, :]
        outs[chunks + 1][...] = outs[0][:margin, :]


def project(
    place, team, tokens, arrays, items, chunk, groups, depth, margin=None, rest=(), wanted=False
):
    count, width = sum(value.shape[0] for value in tokens), tokens[0].shape[1]
    chunks = max(len(parts) for _, parts in items)
    names = sorted({name for _, parts in items for name, _, _ in parts})
    items = [
        (described, [(names.index(n), first, column) for n, first, column in parts])
        for described, parts in items
        if parts
    ]

    def deep_of(listed):
        return sum(depth // (1 if b[2] is None else groups) for d in listed for b in d)

    deep = deep_of([described for described, _ in items])
    copies = sum(len(parts) for _, parts in items)
    kinds = [jnp.bfloat16] * (chunks - bool(rest)) + [jnp.float32] * bool(rest)
    shapes = [jax.ShapeDtypeStruct((count, chunk), kind) for kind in kinds]
    if margin is not None:
        shapes += [jax.ShapeDtypeStruct((margin, chunk), jnp.bfloat16)] * 2
    if wanted:
        shapes.append(jax.ShapeDtypeStruct((count, deep_of(rest)), jnp.bfloat16))
    return pl.pallas_call(
        functools.partial(
            project_kernel,
            items,
            (len(tokens), len(names), wanted),
            chunk,
            margin,
            rest,
            team,
            groups,
            depth,
        ),
        out_shape=shapes,
        in_specs=[IN_SMEM] + [IN_HBM] * (len(tokens) + len(names)),
        out_specs=[IN_VMEM] * len(shapes),
        scratch_shapes=[
            pltpu.VMEM((count, width), jnp.bfloat16),
            pltpu.VMEM((deep, chunks * chunk), jnp.bfloat16),
            pltpu.VMEM((count, chunks * chunk), jnp.float32),
            pltpu.SemaphoreType.DMA((len(tokens) * width // (team * depth),)),
            pltpu.SemaphoreType.DMA((copies,)),
        ],
        compiler_params=PARAMS,
        cost_estimate=cost(
            2 * count * deep * chunks * chunk,
            2 * chunks * chunk * (count + deep) + 2 * count * width,
        ),
        name="project",
    )(place, *tokens, *[arrays[name] for name in names])


def attend_kernel(
    base, block, deep, firsts, first_ref, count_ref, before, own, after, *refs
):
    outs, (window, query) = refs[:-2][-(len(refs) - 2 - firsts[0]) :], refs[-2:]
    ins = refs[: firsts[0]]
    per_out = outs[0].shape[0] // block
    total_blocks = per_out * len(outs)
    mine = pl.ds(base * block, total_blocks * block)
    if deep:
        *sums, left = ins[: len(firsts[1]) + 1]
        weights = iter(ins[len(firsts[1]) + 1 :])
        for c, (begun, starts) in enumerate(zip(sums, firsts[1])):
            total = begun[mine, :]
            for i, start in enumerate(starts):
                total += jnp.dot(
                    left[mine, i * deep : (i + 1) * deep],
                    next(weights)[start : start + deep, :],
                    preferred_element_type=jnp.float32,
                )
            wide = total.shape[1]
            query[:, c * wide : (c + 1) * wide] = total.astype(jnp.bfloat16)
    else:
        query[...] = ins[0][mine, :]
    offset = 0
    for ref in (before, own, after):
        window[offset : offset + ref.shape[0], :] = ref[...]
        offset += ref.shape[0]
    heads = query.shape[1] // HD
    span = MOST_BLK * block
    row = lax.broadcasted_iota(jnp.int32, (span, 1), 0)

    def place_of(b):
        return pl.ds(pl.multiple_of(first_ref[base + b] * block, block), span)

    def score(b):
        rows = pl.ds(b * block, block)
        stacked = jnp.concatenate(
            [query[rows, h * HD : (h + 1) * HD] for h in range(heads)], axis=0
        )
        return lax.dot_general(
            window[place_of(b), :HD],
            stacked,
            (((1,), (1,)), ((), ())),
            preferred_element_type=jnp.float32,
        )

    scores = score(0)
    for b in range(total_blocks):
        upcoming = score(b + 1) if b + 1 < total_blocks else None
        scores = jnp.where(row < count_ref[base + b] * block, scores, -1e30)
        row_max = jnp.max(scores, axis=0, keepdims=True)
        weights = jnp.exp2((scores - row_max) * (HD ** (-0.5) * LOG2_E))
        row_total = jnp.sum(weights, axis=0, keepdims=True)
        mixed = lax.dot_general(
            window[place_of(b), HD:],
            weights.astype(jnp.bfloat16),
            (((0,), (0,)), ((), ())),
            preferred_element_type=jnp.float32,
        )
        mixed = mixed / row_total
        out = outs[b // per_out]
        rows = pl.ds((b % per_out) * block, block)
        for h in range(heads):
            turned = mixed[:, h * block : (h + 1) * block].T
            out[rows, h * HD : (h + 1) * HD] = turned.astype(jnp.bfloat16)
        scores = upcoming


def attend(first, count, query, before, own, after, block, base, rows, parts):
    if isinstance(query, tuple):
        *sums, left, lates = query
        ins = [*sums, left] + [array for late in lates for array, _ in late]
        firsts = (len(ins), [[start for _, start in late] for late in lates])
        deep = left.shape[1] // len(lates[0])
        columns = sum(value.shape[1] for value in sums)
    else:
        ins, firsts, deep, columns = [query], (1, []), 0, query.shape[1]
    span = before.shape[0] + own.shape[0] + after.shape[0]
    return pl.pallas_call(
        functools.partial(attend_kernel, base, block, deep, firsts),
        out_shape=[jax.ShapeDtypeStruct((rows, columns), jnp.bfloat16)] * parts,
        in_specs=[IN_SMEM] * 2 + [IN_VMEM] * (3 + len(ins)),
        out_specs=[IN_VMEM] * parts,
        scratch_shapes=[
            pltpu.VMEM((span, own.shape[1]), jnp.bfloat16),
            pltpu.VMEM((parts * rows, columns), jnp.bfloat16),
        ],
        compiler_params=PARAMS,
        cost_estimate=cost(
            4 * parts * rows * MOST_BLK * block * columns,
            4 * rows * columns + 2 * span * own.shape[1],
            parts * rows * MOST_BLK * block * (columns // HD),
        ),
        name="attend",
    )(first, count, before, own, after, *ins)


def assemble_kernel(place, *refs):
    pieces, out = refs[:-1], refs[-1]
    for r, piece in enumerate(pieces):
        width = piece.shape[1]
        first = pl.multiple_of((place[2] ^ r) * width, width)
        out[:, pl.ds(first, width)] = piece[...]


def assemble(place, pieces):
    rows, width = pieces[0].shape
    return pl.pallas_call(
        assemble_kernel,
        out_shape=jax.ShapeDtypeStruct((rows, width * len(pieces)), jnp.bfloat16),
        in_specs=[IN_SMEM] + [IN_VMEM] * len(pieces),
        out_specs=IN_VMEM,
        compiler_params=PARAMS,
        cost_estimate=cost(0, 4 * rows * width * len(pieces)),
        name="assemble",
    )(place, *pieces)


def on_device(tokens, norm_gain, w_query, w_key, w_value, passage_blocks):
    groups, peers = lax.axis_size("groups"), lax.axis_size("seq")
    team = w_key.shape[1] // HD
    layers = peers // team
    depth = w_key.shape[0]
    rows = tokens.shape[0]
    blocks = passage_blocks.shape[0]
    block = rows // blocks
    index = lax.axis_index("seq")
    group, layer, member = lax.axis_index("groups"), index // team, index % team
    place = jnp.stack([group, layer, member]).astype(jnp.int32)
    widths = [2 * HD] * ((w_key.shape[1] + w_value.shape[1] + w_query.shape[1]) // (2 * HD * team))
    margin = (MOST_BLK - 1) * block

    if depth // groups % LANES == 0 and team * blocks <= NOTES:
        chunk = 2 * HD
        packed = pack(place, passage_blocks, [w_key, w_value, w_query], team, groups)
        moved = [swap(packed[r], team, 0, 0, r) for r in range(1, team)]
        steps = range(1, 2)
        lengths = [rows]
        normed = normalize(tie(tokens, packed[0]), norm_gain, lengths)
        *shards, far = make_shards(
            tie(place, normed[0]), packed[0], moved, widths, depth, groups, blocks
        )

        chunks = len(shards)
        hops = max(bits.bit_count() for bits in range(layers))
        arrays = {"own": packed[0], "far": far}
        arrays.update({f"normed{i}": value for i, value in zip(steps, normed)})
        arrays.update({f"moved{r}": value for r, value in enumerate(moved, 1)})
        arrays.update({f"shard{c}": shard for c, shard in enumerate(shards)})
        held = {(c, 0): (f"shard{c}", 0, shard.shape[0]) for c, shard in enumerate(shards)}
        crossed, far_tokens, diagonal = {}, [], []
        part = depth // groups

        def join(parts):
            views = [arrays[name][first : first + n] for name, first, n in parts]
            return views[0] if len(views) == 1 else jnp.concatenate(views, axis=0)

        def items_of(cs, layer_bits=range(layers), others=range(groups)):
            items = []
            if 0 in layer_bits:
                for r, name in enumerate(["own"] + [f"moved{r}" for r in range(1, team)]):
                    described = [(0, r, None if r < 2 else 0)]
                    items.append((described, [(name, 0, c * chunk) for c in cs]))
                for other in range(1, groups):
                    described = [(0, r, other) for r in range(2, team)]
                    items.append((described, [(f"far{other}", 0, c * chunk) for c in cs]))
            for other in others:
                for bits in layer_bits:
                    if bits:
                        described = [(bits, r, other) for r in range(team)]
                        where = [crossed[c, bits, other] if other else held[c, bits] for c in cs]
                        items.append((described, [(n, first, 0) for n, first, _ in where]))
            return items

        hardest = [bits for bits in range(layers) if bits.bit_count() == hops]

        def without_last(cs):
            items, rest, late = [], [], []
            for described, parts in items_of(cs):
                if described[0][2] and described[0][0] in hardest:
                    name, first, _ = parts[-1]
                    late.append((name, first))
                    rest.append(described)
                    parts = parts[:-1]
                items.append((described, parts))
            late = [(arrays[n], f) for n, f in late if n in arrays]
            return items, rest, late

        for phase in range(1, chunks + hops + 1):
            long = arrays.pop("tokens1", None) if phase < chunks + hops - 1 else None
            if phase < chunks + hops:
                arrays = lax.optimization_barrier(arrays)
            if long is not None:
                arrays["tokens1"] = long
            sends = []
            ways = {}
            for c in range(chunks):
                for bits in range(1, layers):
                    low = bits & -bits
                    if c + bits.bit_count() == phase:
                        ways.setdefault((0, low), []).append((c, bits, held[c, bits ^ low]))
                    elif c + bits.bit_count() + 1 == phase:
                        for other in range(1, groups):
                            way = ways.setdefault((other, 0), [])
                            way.append((c, bits, held[c, bits]))
            for (other, low), listed in ways.items():
                name = f"phase{phase}from{other}{low}"
                value = join([p for _, _, p in listed])
                sends.append((other, low, 0, name, value))
                first = 0
                for c, bits, (_, _, n) in listed:
                    if other:
                        crossed[c, bits, other] = (name, first, n)
                    else:
                        held[c, bits] = (name, first, n)
                    first += n
            if phase in steps:
                sends.append((0, 0, 2, f"tokens{phase}", arrays[f"normed{phase}"]))
            if phase == chunks + hops - 1:
                sends.append((0, 0, 1, "diagonal1", arrays["tokens1"]))
            if phase == 1:
                for i in steps:
                    sends.append((0, 0, 1, f"near{i}", arrays[f"normed{i}"]))
                for other in range(1, groups):
                    sends.append((other, 0, 0, f"far{other}", arrays["far"]))
            new = {}
            for group_bits, layer_bits, member_bits, name, value in sends:
                new[name] = swap(value, team, group_bits, layer_bits, member_bits)
            arrays.update(new)
            if phase == chunks + hops - 1:
                team_tokens = [arrays[f"normed{i}"] for i in steps]
                team_tokens += [arrays[f"near{i}"] for i in steps]
                team_tokens += [arrays[f"tokens{i}"] for i in steps]
                team_tokens += [arrays[f"diagonal{i}"] for i in steps]
                items, rest, _ = without_last(range(chunks - 1))
                made = project(
                    place,
                    team,
                    team_tokens,
                    arrays,
                    items,
                    chunk,
                    groups,
                    depth,
                    margin,
                    rest,
                    True,
                )
                names = ["keys_values"] + [f"sum{c}" for c in range(1, chunks - 1)]
                arrays.update(zip(names + ["tail", "head", "left"], made))
        team_tokens = [arrays[f"normed{i}"] for i in steps]
        team_tokens += [arrays[f"near{i}"] for i in steps]
        team_tokens += [arrays[f"tokens{i}"] for i in steps]
        team_tokens += [arrays[f"diagonal{i}"] for i in steps]
        keys_values, tail, head = (arrays[n] for n in ("keys_values", "tail", "head"))
        items, rest, late = without_last([chunks - 1])
        (begun,) = project(
            place, team, team_tokens, arrays, items, chunk, groups, depth, rest=rest
        )
        lates = [without_last([chunks - 2])[2], late]
        query = (arrays[f"sum{chunks - 2}"], begun, arrays["left"], lates)
        assert chunks == 3
        ids = []
        for s in range(layers):
            name, first, n = held[0, s]
            noted = arrays[name][first + team * part : first + n]
            ids.append(noted[: team * blocks, 0])
        ids = jnp.stack(ids).astype(jnp.int32)
        mine = ids[0]
        ids = ids.reshape(-1)
    else:
        (normed,) = normalize(tokens, norm_gain, [rows])
        team_tokens = [normed] + [swap(normed, team, 0, 0, r) for r in range(1, team)]
        stacked = jnp.stack(team_tokens)
        in_order = jnp.concatenate(
            [lax.dynamic_index_in_dim(stacked, member ^ t, 0, False) for t in range(team)]
        )

        def dense(weight, rows_of_tokens):
            whole = lax.all_gather(weight, "seq", axis=0, tiled=True)
            width = weight.shape[1] // team
            own = lax.dynamic_slice_in_dim(whole, member * width, width, 1)
            product = jnp.dot(rows_of_tokens, own, preferred_element_type=jnp.float32)
            return product.astype(jnp.bfloat16)

        keys_values = jnp.concatenate(
            [dense(w_key, in_order), dense(w_value, in_order)], axis=1
        )
        tail, head = keys_values[-margin:], keys_values[:margin]
        query = dense(w_query, stacked.reshape(team * rows, tokens.shape[1]))
        ids = lax.all_gather(passage_blocks, "seq", axis=0, tiled=True)
        mine = jnp.concatenate(
            [
                lax.dynamic_slice_in_dim(ids, (layer * team + (member ^ r)) * blocks, blocks)
                for r in range(team)
            ]
        )

    before = from_layer(tail, team, -1)
    after = from_layer(head, team, 1)

    count = jnp.sum((mine[:, None] == ids[None, :]).astype(jnp.int32), axis=1)
    first = jnp.sum((ids[None, :] < mine[:, None]).astype(jnp.int32), axis=1)
    first = first - layer * team * blocks + (MOST_BLK - 1)

    pieces = [None] * team
    for start, end in ((1, team), (0, 1)):
        made = attend(
            first,
            count,
            query,
            before,
            keys_values,
            after,
            block,
            start * blocks,
            rows,
            end - start,
        )
        for r, piece in enumerate(made, start):
            pieces[r] = swap(piece, team, 0, 0, r) if r else piece
    return assemble(place, pieces)


def solution(mesh):
    in_specs = (
        P(("groups", "seq"), None),
        P(),
        P("seq", None),
        P("seq", None),
        P("seq", None),
        P(("groups", "seq")),
    )
    out_specs = P(("groups", "seq"), None)
    return jax.shard_map(
        on_device, mesh=mesh, in_specs=in_specs, out_specs=out_specs, check_vma=False
    )
```

```python
import functools

import jax
import jax.numpy as jnp
from jax import lax
from jax.experimental import pallas as pl
from jax.experimental.pallas import tpu as pltpu
from jax.sharding import PartitionSpec as P

HD = 128
MOST_BLK = 7
LANES = 128
NOTES = 16
LONG = ("normed", "far_tokens")
AXES = ("groups", "seq")
LOG2_E = 1.4426950408889634
VMEM_LIMIT = 64 * 1024 * 1024
IN_VMEM = pl.BlockSpec(memory_space=pltpu.VMEM)
IN_SMEM = pl.BlockSpec(memory_space=pltpu.SMEM)
IN_HBM = pl.BlockSpec(memory_space=pltpu.HBM)
PARAMS = pltpu.CompilerParams(vmem_limit_bytes=VMEM_LIMIT)


def cost(flops, size, transcendentals=0):
    return pl.CostEstimate(
        flops=flops, bytes_accessed=size, transcendentals=transcendentals
    )


def swap(value, team, group_bits, layer_bits, member_bits):
    groups, peers = lax.axis_size("groups"), lax.axis_size("seq")
    pairs = []
    for g in range(groups):
        for s in range(peers):
            layer, member = divmod(s, team)
            to = (layer ^ layer_bits) * team + (member ^ member_bits)
            pairs.append((g * peers + s, (g ^ group_bits) * peers + to))
    return lax.ppermute(value, AXES, pairs)


def from_layer(value, team, by):
    groups, peers = lax.axis_size("groups"), lax.axis_size("seq")
    pairs = []
    for g in range(groups):
        for s in range(peers):
            to = s - by * team
            if 0 <= to < peers:
                pairs.append((g * peers + s, g * peers + to))
    return lax.ppermute(value, AXES, pairs)


def tie(value, *others):
    return lax.optimization_barrier((value,) + others)[0] if others else value


def norm_kernel(tokens_ref, gain_ref, *outs):
    first = 0
    for out in outs:
        widened = tokens_ref[first : first + out.shape[0], :].astype(jnp.float32)
        square = jnp.mean(widened * widened, axis=-1, keepdims=True)
        out[...] = (widened * lax.rsqrt(square + 1e-05) * gain_ref[...]).astype(jnp.bfloat16)
        first += out.shape[0]


def normalize(tokens, norm_gain, lengths):
    rows, width = tokens.shape
    return pl.pallas_call(
        norm_kernel,
        out_shape=[jax.ShapeDtypeStruct((n, width), jnp.bfloat16) for n in lengths],
        in_specs=[IN_VMEM] * 2,
        out_specs=[IN_VMEM] * len(lengths),
        compiler_params=PARAMS,
        cost_estimate=cost(6 * rows * width, 4 * rows * width, rows),
        name="normalize",
    )(tokens, norm_gain.reshape(1, width))


def pack_kernel(team, part, notes, count, place, numbers, *refs):
    weights, outs = refs[:count], refs[count : count + team]
    loaded, sems = refs[count + team : -1], refs[-1]
    copies = [
        pltpu.make_async_copy(weight, there, sems.at[i])
        for i, (weight, there) in enumerate(zip(weights, loaded))
    ]
    for copy in copies:
        copy.start()
    if notes:
        row = lax.broadcasted_iota(jnp.int32, (notes, outs[0].shape[1]), 0)
        noted = jnp.zeros((notes, outs[0].shape[1]), jnp.float32)
        for i in range(numbers.shape[0]):
            noted = jnp.where(row == i, numbers[i].astype(jnp.float32), noted)
        noted = noted.astype(jnp.bfloat16)
        for out in outs:
            out[out.shape[0] - notes :, :] = noted
    column = 0
    for copy, weight in zip(copies, loaded):
        copy.wait()
        width = weight.shape[1] // team
        for r, out in enumerate(outs):
            length = out.shape[0] - notes
            first = 0 if r < 2 else pl.multiple_of(place[0] * part, part)
            columns = pl.ds(pl.multiple_of((place[2] ^ r) * width, width), width)
            out[:length, column : column + width] = weight[pl.ds(first, length), columns]
        column += width


def pack(place, numbers, weights, team, groups, notes=0):
    depth = weights[0].shape[0]
    width = sum(weight.shape[1] for weight in weights) // team
    lengths = [depth if r < 2 else depth // groups for r in range(team)]
    return pl.pallas_call(
        functools.partial(pack_kernel, team, depth // groups, notes, len(weights)),
        out_shape=[
            jax.ShapeDtypeStruct((length + notes, width), jnp.bfloat16)
            for length in lengths
        ],
        in_specs=[IN_SMEM] * 2 + [IN_HBM] * len(weights),
        out_specs=[IN_VMEM] * team,
        scratch_shapes=[pltpu.VMEM(w.shape, w.dtype) for w in weights]
        + [pltpu.SemaphoreType.DMA((len(weights),))],
        compiler_params=PARAMS,
        cost_estimate=cost(0, 4 * team * depth * width),
        name="pack",
    )(place, numbers, *weights)


def shards_kernel(team, part, blocks, place, *refs):
    ins, shards, far = refs[:team], refs[team:-1], refs[-1]
    mine = pl.ds(pl.multiple_of(place[0] * part, part), part)
    for r, ref in enumerate(ins):
        rows = mine if r < 2 else pl.ds(0, part)
        column = 0
        for shard in shards:
            width = shard.shape[1]
            shard[r * part : (r + 1) * part, :] = ref[rows, column : column + width]
            column += width
        if r >= 2:
            far[(r - 2) * part : (r - 1) * part, :] = ref[rows, :]
    if not blocks:
        return
    noted_in = shards[0]
    row = lax.broadcasted_iota(jnp.int32, (NOTES, noted_in.shape[1]), 0)
    noted = jnp.zeros((NOTES, noted_in.shape[1]), jnp.float32)
    for r, ref in enumerate(ins):
        held = ref[ref.shape[0] - NOTES :, : noted_in.shape[1]].astype(jnp.float32)
        for i in range(blocks):
            noted = jnp.where(row == r * blocks + i, held[i : i + 1, :], noted)
    noted_in[team * part :, :] = noted.astype(jnp.bfloat16)


def make_shards(place, packed, moved, widths, depth, groups, blocks=0):
    part, width = depth // groups, packed.shape[1]
    team = 1 + len(moved)
    shapes = [(team * part + (NOTES if blocks and not i else 0), w) for i, w in enumerate(widths)]
    shapes.append(((team - 2) * part, width))
    return pl.pallas_call(
        functools.partial(shards_kernel, team, part, blocks),
        out_shape=[jax.ShapeDtypeStruct(shape, jnp.bfloat16) for shape in shapes],
        in_specs=[IN_SMEM] + [IN_VMEM] * team,
        out_specs=[IN_VMEM] * len(shapes),
        compiler_params=PARAMS,
        cost_estimate=cost(0, 6 * team * part * width),
        name="shards",
    )(place, packed, *moved)


def project_kernel(items, counts, chunk, margin, rest, team, groups, depth, place, *refs):
    held, arrays, wanted = counts
    sources, refs = refs[:held], refs[held:]
    stored, refs = refs[:arrays], refs[arrays:]
    outs, (tokens, weights, total, token_sems, sems) = refs[:-5], refs[-5:]
    part = depth // groups
    group, layer, member = place[0], place[1], place[2]
    layer_wide = team * depth
    layers = sorted({described[0][0] for described, _ in items})
    plan, offset, copies, token_copies = [], 0, 0, 0
    for layer_bits in layers:
        loads, matched, row = [], [], 0
        first = pl.multiple_of((layer ^ layer_bits) * layer_wide, LANES)
        for ref in sources:
            here = pl.ds(first, layer_wide)
            there = tokens.at[pl.ds(row, ref.shape[0]), here]
            loads.append(
                pltpu.make_async_copy(ref.at[:, here], there, token_sems.at[token_copies])
            )
            row += ref.shape[0]
            token_copies += 1
        for described, parts in items:
            if described[0][0] != layer_bits:
                continue
            deep = sum(depth if bits[2] is None else part for bits in described)
            for c, (source, first, column) in enumerate(parts):
                loads.append(
                    pltpu.make_async_copy(
                        stored[source].at[pl.ds(first, deep), pl.ds(column, chunk)],
                        weights.at[pl.ds(offset, deep), pl.ds(c * chunk, chunk)],
                        sems.at[copies],
                    )
                )
                copies += 1
            matched.append((described, offset, deep, len(parts) * chunk))
            offset += deep
        for copy in loads:
            copy.start()
        plan.append((loads, matched))

    def columns_of(own, described):
        lefts = []
        for layer_bits, member_bits, group_bits in described:
            owner = (layer ^ layer_bits) * team + (member ^ member_bits)
            first, wide = owner * depth, depth
            if group_bits is not None:
                first, wide = first + (group ^ group_bits) * part, part
            lefts.append(tokens[own, pl.ds(pl.multiple_of(first, LANES), wide)])
        return lefts[0] if len(lefts) == 1 else jnp.concatenate(lefts, axis=1)

    span = tokens.shape[0] // 2
    for step, (loads, matched) in enumerate(plan):
        for copy in loads:
            copy.wait()
        for half in range(2):
            own = pl.ds(half * span, span)
            for i, (described, offset, deep, wide) in enumerate(matched):
                right = weights[pl.ds(offset, deep), :wide]
                term = jnp.dot(
                    columns_of(own, described), right, preferred_element_type=jnp.float32
                )
                if i == 0 and step == 0:
                    total[own, :wide] = term
                else:
                    total[own, :wide] += term
    if wanted:
        column = 0
        for described in rest:
            left = columns_of(pl.ds(0, tokens.shape[0]), described)
            outs[-1][:, column : column + left.shape[1]] = left
            column += left.shape[1]
    rows = total.shape[0] // team
    chunks = total.shape[1] // chunk
    for c in range(chunks):
        columns = slice(c * chunk, (c + 1) * chunk)
        if rest and c + 1 == chunks:
            outs[c][...] = total[:, columns]
            continue
        for r in range(team):
            first = r * rows
            if c == 0 and margin is not None:
                first = pl.multiple_of((member ^ r) * rows, rows)
            made = total[r * rows : (r + 1) * rows, columns]
            outs[c][pl.ds(first, rows), :] = made.astype(jnp.bfloat16)
    if margin is not None:
        outs[chunks][...] = outs[0][total.shape[0] - margin :, :]
        outs[chunks + 1][...] = outs[0][:margin, :]


def project(
    place, team, tokens, arrays, items, chunk, groups, depth, margin=None, rest=(), wanted=False
):
    count, width = sum(value.shape[0] for value in tokens), tokens[0].shape[1]
    chunks = max(len(parts) for _, parts in items)
    names = sorted({name for _, parts in items for name, _, _ in parts})
    items = [
        (described, [(names.index(n), first, column) for n, first, column in parts])
        for described, parts in items
        if parts
    ]

    def deep_of(listed):
        return sum(depth // (1 if b[2] is None else groups) for d in listed for b in d)

    deep = deep_of([described for described, _ in items])
    copies = sum(len(parts) for _, parts in items)
    kinds = [jnp.bfloat16] * (chunks - bool(rest)) + [jnp.float32] * bool(rest)
    shapes = [jax.ShapeDtypeStruct((count, chunk), kind) for kind in kinds]
    if margin is not None:
        shapes += [jax.ShapeDtypeStruct((margin, chunk), jnp.bfloat16)] * 2
    if wanted:
        shapes.append(jax.ShapeDtypeStruct((count, deep_of(rest)), jnp.bfloat16))
    return pl.pallas_call(
        functools.partial(
            project_kernel,
            items,
            (len(tokens), len(names), wanted),
            chunk,
            margin,
            rest,
            team,
            groups,
            depth,
        ),
        out_shape=shapes,
        in_specs=[IN_SMEM] + [IN_HBM] * (len(tokens) + len(names)),
        out_specs=[IN_VMEM] * len(shapes),
        scratch_shapes=[
            pltpu.VMEM((count, width), jnp.bfloat16),
            pltpu.VMEM((deep, chunks * chunk), jnp.bfloat16),
            pltpu.VMEM((count, chunks * chunk), jnp.float32),
            pltpu.SemaphoreType.DMA((len(tokens) * width // (team * depth),)),
            pltpu.SemaphoreType.DMA((copies,)),
        ],
        compiler_params=PARAMS,
        cost_estimate=cost(
            2 * count * deep * chunks * chunk,
            2 * chunks * chunk * (count + deep) + 2 * count * width,
        ),
        name="project",
    )(place, *tokens, *[arrays[name] for name in names])


def places_kernel(blocks, firsts, place, *refs):
    ins, (first, count), (held, sems) = refs[:-4], refs[-4:-2], refs[-2:]
    copies = []
    for i, (ref, start) in enumerate(zip(ins, firsts)):
        there = held.at[pl.ds(i * NOTES, NOTES)]
        copies.append(pltpu.make_async_copy(ref.at[pl.ds(start, NOTES)], there, sems.at[i]))
        copies[-1].start()
    for copy in copies:
        copy.wait()
    ids = held[:, :LANES].astype(jnp.float32)
    mine = ids[:NOTES]
    same, less = jnp.zeros_like(mine), jnp.zeros_like(mine)
    for i in range(len(ins)):
        for k in range(blocks):
            other = ids[i * NOTES + k : i * NOTES + k + 1]
            same += (other == mine).astype(jnp.float32)
            less += (other < mine).astype(jnp.float32)
    count[...] = same.astype(jnp.int32)
    first[...] = less.astype(jnp.int32) - place[1] * blocks + (MOST_BLK - 1)


def places(place, noted, blocks):
    shape = jax.ShapeDtypeStruct((NOTES, LANES), jnp.int32)
    width = noted[0][0].shape[1]
    first, count = pl.pallas_call(
        functools.partial(places_kernel, blocks, [start for _, start in noted]),
        out_shape=[shape] * 2,
        in_specs=[IN_SMEM] + [IN_HBM] * len(noted),
        out_specs=[IN_VMEM] * 2,
        scratch_shapes=[
            pltpu.VMEM((len(noted) * NOTES, width), jnp.bfloat16),
            pltpu.SemaphoreType.DMA((len(noted),)),
        ],
        compiler_params=PARAMS,
        cost_estimate=cost(0, 4 * NOTES * width * len(noted)),
        name="places",
    )(place, *[array for array, _ in noted])
    return first, count


def attend_kernel(
    base, block, deep, firsts, first_ref, count_ref, before, own, after, *refs
):
    outs, (window, query) = refs[:-2][-(len(refs) - 2 - firsts[0]) :], refs[-2:]
    ins = refs[: firsts[0]]
    per_out = outs[0].shape[0] // block
    total_blocks = per_out * len(outs)
    mine = pl.ds(base * block, total_blocks * block)
    column = 0
    for ref in ins[: firsts[0] - (2 + len(firsts[1]) if deep else 0)]:
        query[:, column : column + ref.shape[1]] = ref[mine, :]
        column += ref.shape[1]
    if deep:
        begun, left, *weights = ins[firsts[0] - 2 - len(firsts[1]) :]
        total = begun[mine, :]
        for i, (weight, start) in enumerate(zip(weights, firsts[1])):
            total += jnp.dot(
                left[mine, i * deep : (i + 1) * deep],
                weight[start : start + deep, :],
                preferred_element_type=jnp.float32,
            )
        query[:, column:] = total.astype(jnp.bfloat16)
    offset = 0
    for ref in (before, own, after):
        window[offset : offset + ref.shape[0], :] = ref[...]
        offset += ref.shape[0]
    heads = query.shape[1] // HD
    span = MOST_BLK * block
    row = lax.broadcasted_iota(jnp.int32, (span, 1), 0)

    def place_of(b):
        return pl.ds(pl.multiple_of(first_ref[base + b, 0] * block, block), span)

    def score(b):
        rows = pl.ds(b * block, block)
        stacked = jnp.concatenate(
            [query[rows, h * HD : (h + 1) * HD] for h in range(heads)], axis=0
        )
        return lax.dot_general(
            window[place_of(b), :HD],
            stacked,
            (((1,), (1,)), ((), ())),
            preferred_element_type=jnp.float32,
        )

    scores = score(0)
    for b in range(total_blocks):
        upcoming = score(b + 1) if b + 1 < total_blocks else None
        scores = jnp.where(row < count_ref[base + b, 0] * block, scores, -1e30)
        row_max = jnp.max(scores, axis=0, keepdims=True)
        weights = jnp.exp2((scores - row_max) * (HD ** (-0.5) * LOG2_E))
        row_total = jnp.sum(weights, axis=0, keepdims=True)
        mixed = lax.dot_general(
            window[place_of(b), HD:],
            weights.astype(jnp.bfloat16),
            (((0,), (0,)), ((), ())),
            preferred_element_type=jnp.float32,
        )
        mixed = mixed / row_total
        out = outs[b // per_out]
        rows = pl.ds((b % per_out) * block, block)
        for h in range(heads):
            turned = mixed[:, h * block : (h + 1) * block].T
            out[rows, h * HD : (h + 1) * HD] = turned.astype(jnp.bfloat16)
        scores = upcoming


def attend(first, count, query, before, own, after, block, base, rows, parts):
    if isinstance(query, tuple):
        done, begun, left, late = query
        ins = [*done, begun, left] + [array for array, _ in late]
        firsts = (len(ins), [start for _, start in late])
        deep = left.shape[1] // len(late)
        columns = sum(value.shape[1] for value in done) + begun.shape[1]
    else:
        ins, firsts, deep, columns = [query], (1, []), 0, query.shape[1]
    span = before.shape[0] + own.shape[0] + after.shape[0]
    return pl.pallas_call(
        functools.partial(attend_kernel, base, block, deep, firsts),
        out_shape=[jax.ShapeDtypeStruct((rows, columns), jnp.bfloat16)] * parts,
        in_specs=[IN_SMEM] * 2 + [IN_VMEM] * (3 + len(ins)),
        out_specs=[IN_VMEM] * parts,
        scratch_shapes=[
            pltpu.VMEM((span, own.shape[1]), jnp.bfloat16),
            pltpu.VMEM((parts * rows, columns), jnp.bfloat16),
        ],
        compiler_params=PARAMS,
        cost_estimate=cost(
            4 * parts * rows * MOST_BLK * block * columns,
            4 * rows * columns + 2 * span * own.shape[1],
            parts * rows * MOST_BLK * block * (columns // HD),
        ),
        name="attend",
    )(first, count, before, own, after, *ins)


def on_device(tokens, norm_gain, w_query, w_key, w_value, passage_blocks):
    groups, peers = lax.axis_size("groups"), lax.axis_size("seq")
    team = w_key.shape[1] // HD
    layers = peers // team
    depth = w_key.shape[0]
    rows = tokens.shape[0]
    blocks = passage_blocks.shape[0]
    block = rows // blocks
    index = lax.axis_index("seq")
    group, layer, member = lax.axis_index("groups"), index // team, index % team
    place = jnp.stack([group, layer, member]).astype(jnp.int32)
    widths = [2 * HD] * ((w_key.shape[1] + w_value.shape[1] + w_query.shape[1]) // (2 * HD * team))
    margin = (MOST_BLK - 1) * block

    if depth // groups % LANES == 0 and team * blocks <= NOTES:
        chunk = 2 * HD
        weights = [w_key, w_value, w_query]
        packed = pack(place, passage_blocks, weights, team, groups, NOTES)
        moved = [swap(packed[r], team, 0, 0, r) for r in range(1, team)]
        (normed,) = normalize(tie(tokens, packed[0]), norm_gain, [rows])
        *shards, far = make_shards(
            tie(place, normed), packed[0], moved, widths, depth, groups, blocks
        )

        chunks = len(shards)
        hops = max(bits.bit_count() for bits in range(layers))
        arrays = {"layer0": packed[0], "far": far, "normed": normed}
        arrays["far_tokens"] = swap(tie(normed, *moved[1:]), team, 0, 0, 2)
        arrays.update({f"layer{r}": value for r, value in enumerate(moved, 1)})
        arrays.update({f"shard{c}": shard for c, shard in enumerate(shards)})
        held = {(c, 0): (f"shard{c}", 0, shard.shape[0]) for c, shard in enumerate(shards)}
        crossed, received = {}, {}
        part = depth // groups

        def join(parts):
            views = [arrays[name][first : first + n] for name, first, n in parts]
            return views[0] if len(views) == 1 else jnp.concatenate(views, axis=0)

        def items_of(cs, layer_bits=range(layers), others=range(groups)):
            items = []
            if 0 in layer_bits:
                for r in range(team):
                    described = [(0, r, None if r < 2 else 0)]
                    items.append((described, [(f"layer{r}", 0, c * chunk) for c in cs]))
                for other in range(1, groups):
                    described = [(0, r, other) for r in range(2, team)]
                    items.append((described, [(f"far{other}", 0, c * chunk) for c in cs]))
            for other in others:
                for bits in layer_bits:
                    if bits:
                        described = [(bits, r, other) for r in range(team)]
                        where = [crossed[c, bits, other] if other else held[c, bits] for c in cs]
                        items.append((described, [(n, first, 0) for n, first, _ in where]))
            return items

        hardest = [bits for bits in range(layers) if bits.bit_count() == hops]

        def without_last(cs):
            items, rest, late = [], [], []
            for described, parts in items_of(cs):
                if described[0][2] and described[0][0] in hardest:
                    name, first, _ = parts[-1]
                    late.append((name, first))
                    rest.append(described)
                    parts = parts[:-1]
                items.append((described, parts))
            late = [(arrays[n], f) for n, f in late if n in arrays]
            return items, rest, late

        for phase in range(1, chunks + hops + 1):
            waited = phase == chunks + hops - 1
            long = {} if waited else {n: arrays.pop(n) for n in LONG if n in arrays}
            if phase < chunks + hops:
                arrays = lax.optimization_barrier(arrays)
            arrays.update(long)
            sends = []
            ways = {}
            for c in range(chunks):
                for bits in range(1, layers):
                    low = bits & -bits
                    if c + bits.bit_count() == phase:
                        ways.setdefault((0, low), []).append((c, bits, held[c, bits ^ low]))
            if waited:
                sends.append((0, 0, 1, "diagonal", arrays["far_tokens"]))
            for name, listed in received.items():
                for other in range(1, groups):
                    value = tie(arrays[name], *[arrays[n] for n in ("tail",) if n in arrays])
                    sends.append((other, 0, 0, f"{name}_{other}", value))
                    for c, bits in listed:
                        _, first, n = held[c, bits]
                        crossed[c, bits, other] = (f"{name}_{other}", first, n)
            received = {}
            for (other, low), listed in ways.items():
                name = f"phase{phase}from{low}"
                value = join([p for _, _, p in listed])
                sends.append((other, low, 0, name, value))
                received[name] = [(c, bits) for c, bits, _ in listed]
                first = 0
                for c, bits, (_, _, n) in listed:
                    held[c, bits] = (name, first, n)
                    first += n
            if phase == 1:
                sends.append((0, 0, 1, "near", tie(normed, arrays["layer0"])))
                for other in range(1, groups):
                    sends.append((other, 0, 0, f"far{other}", arrays["far"]))
            if phase == hops + 1:
                noted = []
                for bits in range(layers):
                    name, start, _ = held[0, bits]
                    noted.append((arrays[name], start + team * part))
                arrays["first"], arrays["count"] = places(place, noted, team * blocks)
            new = {}
            for group_bits, layer_bits, member_bits, name, value in sends:
                new[name] = swap(value, team, group_bits, layer_bits, member_bits)
            arrays.update(new)
            if phase == chunks + hops - 1:
                names = ("normed", "near", "far_tokens", "diagonal")
                team_tokens = [arrays[n] for n in names]
                made = project(
                    place, team, team_tokens, arrays, items_of([0]), chunk, groups, depth, margin
                )
                arrays.update(zip(("keys_values", "tail", "head"), made))
        keys_values, tail, head = (arrays[n] for n in ("keys_values", "tail", "head"))
        items, rest, late = without_last(range(1, chunks))
        *query, begun, left = project(
            place,
            team,
            team_tokens,
            arrays,
            items,
            chunk,
            groups,
            depth,
            rest=rest,
            wanted=True,
        )
        query = (query, begun, left, late)
        first, count = arrays["first"], arrays["count"]
    else:
        (normed,) = normalize(tokens, norm_gain, [rows])
        team_tokens = [normed] + [swap(normed, team, 0, 0, r) for r in range(1, team)]
        stacked = jnp.stack(team_tokens)
        in_order = jnp.concatenate(
            [lax.dynamic_index_in_dim(stacked, member ^ t, 0, False) for t in range(team)]
        )

        def dense(weight, rows_of_tokens):
            whole = lax.all_gather(weight, "seq", axis=0, tiled=True)
            width = weight.shape[1] // team
            own = lax.dynamic_slice_in_dim(whole, member * width, width, 1)
            product = jnp.dot(rows_of_tokens, own, preferred_element_type=jnp.float32)
            return product.astype(jnp.bfloat16)

        keys_values = jnp.concatenate(
            [dense(w_key, in_order), dense(w_value, in_order)], axis=1
        )
        tail, head = keys_values[-margin:], keys_values[:margin]
        query = dense(w_query, stacked.reshape(team * rows, tokens.shape[1]))
        ids = lax.all_gather(passage_blocks, "seq", axis=0, tiled=True)
        mine = jnp.concatenate(
            [
                lax.dynamic_slice_in_dim(ids, (layer * team + (member ^ r)) * blocks, blocks)
                for r in range(team)
            ]
        )

        count = jnp.sum((mine[:, None] == ids[None, :]).astype(jnp.int32), axis=1)
        first = jnp.sum((ids[None, :] < mine[:, None]).astype(jnp.int32), axis=1)
        first = first - layer * team * blocks + (MOST_BLK - 1)
        first, count = first[:, None], count[:, None]

    before = from_layer(tail, team, -1)
    after = from_layer(head, team, 1)

    pieces = [None] * team
    for start, end in ((2, team), (0, 2)):
        made = attend(
            first,
            count,
            query,
            before,
            keys_values,
            after,
            block,
            start * blocks,
            rows,
            end - start,
        )
        for r, piece in enumerate(made, start):
            pieces[r] = swap(piece, team, 0, 0, r) if r else piece
    out = jnp.zeros((rows, w_query.shape[1]), jnp.bfloat16)
    for r in [0, *range(2, team), 1]:
        piece = pieces[r]
        out = lax.dynamic_update_slice(out, piece, (0, (member ^ r) * piece.shape[1]))
    return out


def solution(mesh):
    in_specs = (
        P(("groups", "seq"), None),
        P(),
        P("seq", None),
        P("seq", None),
        P("seq", None),
        P(("groups", "seq")),
    )
    out_specs = P(("groups", "seq"), None)
    return jax.shard_map(
        on_device, mesh=mesh, in_specs=in_specs, out_specs=out_specs, check_vma=False
    )
```

```python
import functools

import jax
import jax.numpy as jnp
from jax import lax
from jax.experimental import pallas as pl
from jax.experimental.pallas import tpu as pltpu
from jax.sharding import PartitionSpec as P

HD = 128
MOST_BLK = 7
LANES = 128
NOTES = 16
LONG = ("normed", "far_tokens")
AXES = ("groups", "seq")
LOG2_E = 1.4426950408889634
VMEM_LIMIT = 64 * 1024 * 1024
IN_VMEM = pl.BlockSpec(memory_space=pltpu.VMEM)
IN_SMEM = pl.BlockSpec(memory_space=pltpu.SMEM)
IN_HBM = pl.BlockSpec(memory_space=pltpu.HBM)
PARAMS = pltpu.CompilerParams(vmem_limit_bytes=VMEM_LIMIT)


def cost(flops, size, transcendentals=0):
    return pl.CostEstimate(
        flops=flops, bytes_accessed=size, transcendentals=transcendentals
    )


def swap(value, team, group_bits, layer_bits, member_bits):
    groups, peers = lax.axis_size("groups"), lax.axis_size("seq")
    pairs = []
    for g in range(groups):
        for s in range(peers):
            layer, member = divmod(s, team)
            to = (layer ^ layer_bits) * team + (member ^ member_bits)
            pairs.append((g * peers + s, (g ^ group_bits) * peers + to))
    return lax.ppermute(value, AXES, pairs)


def swap_outward(value, team):
    groups, peers = lax.axis_size("groups"), lax.axis_size("seq")
    pairs = []
    for g in range(groups):
        for s in range(peers):
            to = s + team if s // team % 2 else s - team
            if 0 <= to < peers:
                pairs.append((g * peers + s, g * peers + to))
    return lax.ppermute(value, AXES, pairs)


def tie(value, *others):
    return lax.optimization_barrier((value,) + others)[0] if others else value


def norm_kernel(tokens_ref, gain_ref, *outs):
    first = 0
    for out in outs:
        widened = tokens_ref[first : first + out.shape[0], :].astype(jnp.float32)
        square = jnp.mean(widened * widened, axis=-1, keepdims=True)
        out[...] = (widened * lax.rsqrt(square + 1e-05) * gain_ref[...]).astype(jnp.bfloat16)
        first += out.shape[0]


def normalize(tokens, norm_gain, lengths):
    rows, width = tokens.shape
    return pl.pallas_call(
        norm_kernel,
        out_shape=[jax.ShapeDtypeStruct((n, width), jnp.bfloat16) for n in lengths],
        in_specs=[IN_VMEM] * 2,
        out_specs=[IN_VMEM] * len(lengths),
        compiler_params=PARAMS,
        cost_estimate=cost(6 * rows * width, 4 * rows * width, rows),
        name="normalize",
    )(tokens, norm_gain.reshape(1, width))


def pack_kernel(team, part, notes, count, numbers, *refs):
    group, member = lax.axis_index("groups"), lax.rem(lax.axis_index("seq"), team)
    weights, outs = refs[:count], refs[count : count + team]
    loaded, sems = refs[count + team : -1], refs[-1]
    copies = [
        pltpu.make_async_copy(weight, there, sems.at[i])
        for i, (weight, there) in enumerate(zip(weights, loaded))
    ]
    for copy in copies:
        copy.start()
    if notes:
        row = lax.broadcasted_iota(jnp.int32, (notes, outs[0].shape[1]), 0)
        noted = jnp.zeros((notes, outs[0].shape[1]), jnp.float32)
        for i in range(numbers.shape[0]):
            noted = jnp.where(row == i, numbers[i].astype(jnp.float32), noted)
        noted = noted.astype(jnp.bfloat16)
        for out in outs:
            out[out.shape[0] - notes :, :] = noted
    column = 0
    for copy, weight in zip(copies, loaded):
        copy.wait()
        width = weight.shape[1] // team
        for r, out in enumerate(outs):
            length = out.shape[0] - notes
            first = 0 if r < 2 else pl.multiple_of(group * part, part)
            columns = pl.ds(pl.multiple_of((member ^ r) * width, width), width)
            out[:length, column : column + width] = weight[pl.ds(first, length), columns]
        column += width


def pack(numbers, weights, team, groups, notes=0):
    depth = weights[0].shape[0]
    width = sum(weight.shape[1] for weight in weights) // team
    lengths = [depth if r < 2 else depth // groups for r in range(team)]
    return pl.pallas_call(
        functools.partial(pack_kernel, team, depth // groups, notes, len(weights)),
        out_shape=[
            jax.ShapeDtypeStruct((length + notes, width), jnp.bfloat16)
            for length in lengths
        ],
        in_specs=[IN_SMEM] + [IN_HBM] * len(weights),
        out_specs=[IN_VMEM] * team,
        scratch_shapes=[pltpu.VMEM(w.shape, w.dtype) for w in weights]
        + [pltpu.SemaphoreType.DMA((len(weights),))],
        compiler_params=PARAMS,
        cost_estimate=cost(0, 4 * team * depth * width),
        name="pack",
    )(numbers, *weights)


def shards_kernel(team, part, blocks, place, *refs):
    ins, shards, far = refs[:team], refs[team:-1], refs[-1]
    mine = pl.ds(pl.multiple_of(place[0] * part, part), part)
    for r, ref in enumerate(ins):
        rows = mine if r < 2 else pl.ds(0, part)
        column = 0
        for shard in shards:
            width = shard.shape[1]
            shard[r * part : (r + 1) * part, :] = ref[rows, column : column + width]
            column += width
        if r >= 2:
            far[(r - 2) * part : (r - 1) * part, :] = ref[rows, :]
    if not blocks:
        return
    noted_in = shards[0]
    row = lax.broadcasted_iota(jnp.int32, (NOTES, noted_in.shape[1]), 0)
    noted = jnp.zeros((NOTES, noted_in.shape[1]), jnp.float32)
    for r, ref in enumerate(ins):
        held = ref[ref.shape[0] - NOTES :, : noted_in.shape[1]].astype(jnp.float32)
        for i in range(blocks):
            noted = jnp.where(row == r * blocks + i, held[i : i + 1, :], noted)
    noted_in[team * part :, :] = noted.astype(jnp.bfloat16)


def make_shards(place, packed, moved, widths, depth, groups, blocks=0):
    part, width = depth // groups, packed.shape[1]
    team = 1 + len(moved)
    shapes = [(team * part + (NOTES if blocks and not i else 0), w) for i, w in enumerate(widths)]
    shapes.append(((team - 2) * part, width))
    return pl.pallas_call(
        functools.partial(shards_kernel, team, part, blocks),
        out_shape=[jax.ShapeDtypeStruct(shape, jnp.bfloat16) for shape in shapes],
        in_specs=[IN_SMEM] + [IN_VMEM] * team,
        out_specs=[IN_VMEM] * len(shapes),
        compiler_params=PARAMS,
        cost_estimate=cost(0, 6 * team * part * width),
        name="shards",
    )(place, packed, *moved)


def project_kernel(items, counts, chunk, margin, rest, team, groups, depth, place, *refs):
    held, arrays, wanted, carried = counts
    sources, refs = refs[:held], refs[held:]
    stored, refs = refs[:arrays], refs[arrays:]
    begun, refs = refs[: 2 * carried], refs[2 * carried :]
    outs, (tokens, weights, total, lefts, token_sems, sems) = refs[:-6], refs[-6:]
    part = depth // groups
    span = 2 * sources[0].shape[0]
    if carried:
        near = pl.ds(0, span)
        pairs = [(begun[0], total.at[near]), (begun[1], lefts)]
        carries = [
            pltpu.make_async_copy(*pair, sems.at[sems.shape[0] - 2 + i])
            for i, pair in enumerate(pairs)
        ]
        for copy in carries:
            copy.start()
    group, layer, member = place[0], place[1], place[2]
    layer_wide = team * depth
    layers = sorted({described[0][0] for described, _ in items})
    plan, offset, copies, token_copies = [], 0, 0, 0
    for layer_bits in layers:
        loads, matched, row = [], [], 0
        first = pl.multiple_of((layer ^ layer_bits) * layer_wide, LANES)
        for ref in sources:
            here = pl.ds(first, layer_wide)
            there = tokens.at[pl.ds(row, ref.shape[0]), here]
            loads.append(
                pltpu.make_async_copy(ref.at[:, here], there, token_sems.at[token_copies])
            )
            row += ref.shape[0]
            token_copies += 1
        for described, parts in items:
            if described[0][0] != layer_bits:
                continue
            deep = sum(depth if bits[2] is None else part for bits in described)
            for c, (source, first, column) in enumerate(parts):
                loads.append(
                    pltpu.make_async_copy(
                        stored[source].at[pl.ds(first, deep), pl.ds(column, chunk)],
                        weights.at[pl.ds(offset, deep), pl.ds(c * chunk, chunk)],
                        sems.at[copies],
                    )
                )
                copies += 1
            matched.append((described, offset, deep, len(parts) * chunk))
            offset += deep
        for copy in loads:
            copy.start()
        plan.append((loads, matched))

    def columns_of(own, described):
        lefts = []
        for layer_bits, member_bits, group_bits in described:
            owner = (layer ^ layer_bits) * team + (member ^ member_bits)
            first, wide = owner * depth, depth
            if group_bits is not None:
                first, wide = first + (group ^ group_bits) * part, part
            lefts.append(tokens[own, pl.ds(pl.multiple_of(first, LANES), wide)])
        return lefts[0] if len(lefts) == 1 else jnp.concatenate(lefts, axis=1)

    shift = span if carried else 0
    if carried:
        for copy in carries:
            copy.wait()
    for step, (loads, matched) in enumerate(plan):
        for copy in loads:
            copy.wait()
        for half in range(tokens.shape[0] // span):
            own = pl.ds(half * span, span)
            to = pl.ds(half * span + shift, span)
            for i, (described, offset, deep, wide) in enumerate(matched):
                right = weights[pl.ds(offset, deep), :wide]
                term = jnp.dot(
                    columns_of(own, described), right, preferred_element_type=jnp.float32
                )
                if i == 0 and step == 0:
                    total[to, :wide] = term
                else:
                    total[to, :wide] += term
        if carried:
            column = 0
            for described in rest:
                for other, offset, deep, wide in matched:
                    if other == described:
                        total[near, :wide] += jnp.dot(
                            lefts[:, column : column + deep],
                            weights[pl.ds(offset, deep), :wide],
                            preferred_element_type=jnp.float32,
                        )
                column += sum(depth if bits[2] is None else part for bits in described)
    if wanted:
        column = 0
        for described in rest:
            left = columns_of(pl.ds(0, tokens.shape[0]), described)
            outs[-1][:, column : column + left.shape[1]] = left
            column += left.shape[1]
    rows = total.shape[0] // team
    chunks = total.shape[1] // chunk
    for c in range(chunks):
        columns = slice(c * chunk, (c + 1) * chunk)
        if rest and not carried and c + 1 == chunks:
            outs[c][...] = total[:, columns]
            continue
        for r in range(team):
            first = r * rows
            if c == 0 and margin is not None:
                first = pl.multiple_of((member ^ r) * rows, rows)
            made = total[r * rows : (r + 1) * rows, columns]
            outs[c][pl.ds(first, rows), :] = made.astype(jnp.bfloat16)
    if margin is not None:
        late, odd = total.shape[0] - margin, lax.rem(layer, 2)
        for out, first in ((outs[chunks], (1 - odd) * late), (outs[chunks + 1], odd * late)):
            out[...] = outs[0][pl.ds(pl.multiple_of(first, LANES), margin), :]


def project(
    place,
    team,
    tokens,
    arrays,
    items,
    chunk,
    groups,
    depth,
    margin=None,
    rest=(),
    wanted=False,
    carried=(),
):
    taken, width = sum(value.shape[0] for value in tokens), tokens[0].shape[1]
    count = taken + (carried[0].shape[0] if carried else 0)
    chunks = max(len(parts) for _, parts in items)
    names = sorted({name for _, parts in items for name, _, _ in parts})
    items = [
        (described, [(names.index(n), first, column) for n, first, column in parts])
        for described, parts in items
        if parts
    ]

    def deep_of(listed):
        return sum(depth // (1 if b[2] is None else groups) for d in listed for b in d)

    deep = deep_of([described for described, _ in items])
    copies = sum(len(parts) for _, parts in items)
    lacking = bool(rest) and not carried
    kinds = [jnp.bfloat16] * (chunks - lacking) + [jnp.float32] * lacking
    shapes = [jax.ShapeDtypeStruct((count, chunk), kind) for kind in kinds]
    if margin is not None:
        shapes += [jax.ShapeDtypeStruct((margin, chunk), jnp.bfloat16)] * 2
    if wanted:
        shapes.append(jax.ShapeDtypeStruct((count, deep_of(rest)), jnp.bfloat16))
    return pl.pallas_call(
        functools.partial(
            project_kernel,
            items,
            (len(tokens), len(names), wanted, bool(carried)),
            chunk,
            margin,
            rest,
            team,
            groups,
            depth,
        ),
        out_shape=shapes,
        in_specs=[IN_SMEM] + [IN_HBM] * (len(tokens) + len(names) + len(carried)),
        out_specs=[IN_VMEM] * len(shapes),
        scratch_shapes=[
            pltpu.VMEM((taken, width), jnp.bfloat16),
            pltpu.VMEM((deep, chunks * chunk), jnp.bfloat16),
            pltpu.VMEM((count, chunks * chunk), jnp.float32),
            pltpu.VMEM(carried[1].shape if carried else (NOTES, LANES), jnp.bfloat16),
            pltpu.SemaphoreType.DMA((len(tokens) * width // (team * depth),)),
            pltpu.SemaphoreType.DMA((copies + len(carried),)),
        ],
        compiler_params=PARAMS,
        cost_estimate=cost(
            2 * taken * deep * chunks * chunk,
            2 * chunks * chunk * (count + deep) + 2 * taken * width,
        ),
        name="project",
    )(place, *tokens, *[arrays[name] for name in names], *carried)


def places_kernel(blocks, firsts, place, *refs):
    ins, (first, count), (held, sems) = refs[:-4], refs[-4:-2], refs[-2:]
    copies = []
    for i, (ref, start) in enumerate(zip(ins, firsts)):
        there = held.at[pl.ds(i * NOTES, NOTES)]
        copies.append(pltpu.make_async_copy(ref.at[pl.ds(start, NOTES)], there, sems.at[i]))
        copies[-1].start()
    for copy in copies:
        copy.wait()
    ids = held[:, :LANES].astype(jnp.float32)
    mine = ids[:NOTES]
    same, less = jnp.zeros_like(mine), jnp.zeros_like(mine)
    for i in range(len(ins)):
        for k in range(blocks):
            other = ids[i * NOTES + k : i * NOTES + k + 1]
            same += (other == mine).astype(jnp.float32)
            less += (other < mine).astype(jnp.float32)
    count[...] = same.astype(jnp.int32)
    first[...] = less.astype(jnp.int32) - place[1] * blocks + (MOST_BLK - 1)


def places(place, noted, blocks):
    shape = jax.ShapeDtypeStruct((NOTES, LANES), jnp.int32)
    width = noted[0][0].shape[1]
    first, count = pl.pallas_call(
        functools.partial(places_kernel, blocks, [start for _, start in noted]),
        out_shape=[shape] * 2,
        in_specs=[IN_SMEM] + [IN_HBM] * len(noted),
        out_specs=[IN_VMEM] * 2,
        scratch_shapes=[
            pltpu.VMEM((len(noted) * NOTES, width), jnp.bfloat16),
            pltpu.SemaphoreType.DMA((len(noted),)),
        ],
        compiler_params=PARAMS,
        cost_estimate=cost(0, 4 * NOTES * width * len(noted)),
        name="places",
    )(place, *[array for array, _ in noted])
    return first, count


def attend_kernel(
    base, block, deep, firsts, first_ref, count_ref, place, inner, own, outer, *refs
):
    outs, (window, query) = refs[:-2][-(len(refs) - 2 - firsts[0]) :], refs[-2:]
    ins = refs[: firsts[0]]
    per_out = outs[0].shape[0] // block
    total_blocks = per_out * len(outs)
    column = 0
    for ref in ins[: firsts[0] - (2 + len(firsts[1]) if deep else 0)]:
        query[:, column : column + ref.shape[1]] = ref[...]
        column += ref.shape[1]
    if deep:
        begun, left, *weights = ins[firsts[0] - 2 - len(firsts[1]) :]
        total = begun[...]
        for i, (weight, start) in enumerate(zip(weights, firsts[1])):
            total += jnp.dot(
                left[:, i * deep : (i + 1) * deep],
                weight[start : start + deep, :],
                preferred_element_type=jnp.float32,
            )
        query[:, column:] = total.astype(jnp.bfloat16)
    margin, odd = inner.shape[0], lax.rem(place[1], 2)
    window[margin : margin + own.shape[0], :] = own[...]

    @pl.when(odd == 0)
    def _():
        window[:margin, :] = outer[...]
        window[margin + own.shape[0] :, :] = inner[...]

    @pl.when(odd == 1)
    def _():
        window[:margin, :] = inner[...]
        window[margin + own.shape[0] :, :] = outer[...]

    heads = query.shape[1] // HD
    span = MOST_BLK * block
    row = lax.broadcasted_iota(jnp.int32, (span, 1), 0)

    def place_of(b):
        return pl.ds(pl.multiple_of(first_ref[base + b, 0] * block, block), span)

    def score(b):
        rows = pl.ds(b * block, block)
        stacked = jnp.concatenate(
            [query[rows, h * HD : (h + 1) * HD] for h in range(heads)], axis=0
        )
        return lax.dot_general(
            window[place_of(b), :HD],
            stacked,
            (((1,), (1,)), ((), ())),
            preferred_element_type=jnp.float32,
        )

    scores = score(0)
    for b in range(total_blocks):
        upcoming = score(b + 1) if b + 1 < total_blocks else None
        scores = jnp.where(row < count_ref[base + b, 0] * block, scores, -1e30)
        row_max = jnp.max(scores, axis=0, keepdims=True)
        weights = jnp.exp2((scores - row_max) * (HD ** (-0.5) * LOG2_E))
        row_total = jnp.sum(weights, axis=0, keepdims=True)
        mixed = lax.dot_general(
            window[place_of(b), HD:],
            weights.astype(jnp.bfloat16),
            (((0,), (0,)), ((), ())),
            preferred_element_type=jnp.float32,
        )
        mixed = mixed / row_total
        out = outs[b // per_out]
        rows = pl.ds((b % per_out) * block, block)
        for h in range(heads):
            turned = mixed[:, h * block : (h + 1) * block].T
            out[rows, h * HD : (h + 1) * HD] = turned.astype(jnp.bfloat16)
        scores = upcoming


def attend(first, count, place, query, inner, own, outer, block, base, rows, parts):
    if isinstance(query, tuple):
        done, begun, left, late = query
        ins = [*done, begun, left] + [array for array, _ in late]
        firsts = (len(ins), [start for _, start in late])
        deep = left.shape[1] // len(late)
        columns = sum(value.shape[1] for value in done) + begun.shape[1]
    else:
        ins, firsts, deep, columns = [query], (1, []), 0, query.shape[1]
    span = 2 * inner.shape[0] + own.shape[0]
    size = parts * rows
    by_rows = [value.shape[0] == own.shape[0] and i < len(ins) - len(firsts[1])
               for i, value in enumerate(ins)]
    specs = [
        pl.BlockSpec((size, value.shape[1]), lambda i: (base * block // size, 0))
        if cut else IN_VMEM
        for value, cut in zip(ins, by_rows)
    ]
    return pl.pallas_call(
        functools.partial(attend_kernel, base, block, deep, firsts),
        out_shape=[jax.ShapeDtypeStruct((rows, columns), jnp.bfloat16)] * parts,
        grid=(1,),
        in_specs=[IN_SMEM] * 3 + [IN_VMEM] * 3 + specs,
        out_specs=[IN_VMEM] * parts,
        scratch_shapes=[
            pltpu.VMEM((span, own.shape[1]), jnp.bfloat16),
            pltpu.VMEM((parts * rows, columns), jnp.bfloat16),
        ],
        compiler_params=PARAMS,
        cost_estimate=cost(
            4 * parts * rows * MOST_BLK * block * columns,
            4 * rows * columns + 2 * span * own.shape[1],
            parts * rows * MOST_BLK * block * (columns // HD),
        ),
        name="attend",
    )(first, count, place, inner, own, outer, *ins)


def on_device(tokens, norm_gain, w_query, w_key, w_value, passage_blocks):
    groups, peers = lax.axis_size("groups"), lax.axis_size("seq")
    team = w_key.shape[1] // HD
    layers = peers // team
    depth = w_key.shape[0]
    rows = tokens.shape[0]
    blocks = passage_blocks.shape[0]
    block = rows // blocks
    index = lax.axis_index("seq")
    group, layer, member = lax.axis_index("groups"), index // team, index % team
    place = jnp.stack([group, layer, member]).astype(jnp.int32)
    widths = [2 * HD] * ((w_key.shape[1] + w_value.shape[1] + w_query.shape[1]) // (2 * HD * team))
    margin = (MOST_BLK - 1) * block

    if depth // groups % LANES == 0 and team * blocks <= NOTES:
        chunk = 2 * HD
        weights = [w_key, w_value, w_query]
        packed = pack(passage_blocks, weights, team, groups, NOTES)
        moved = [swap(packed[r], team, 0, 0, r) for r in range(1, team)]
        (normed,) = normalize(tie(tokens, packed[0]), norm_gain, [rows])
        *shards, far = make_shards(
            tie(place, normed), packed[0], moved, widths, depth, groups, blocks
        )

        chunks = len(shards)
        hops = max(bits.bit_count() for bits in range(layers))
        arrays = {"layer0": packed[0], "far": far, "normed": normed}
        arrays["far_tokens"] = swap(tie(normed, *moved[1:]), team, 0, 0, 2)
        arrays.update({f"layer{r}": value for r, value in enumerate(moved, 1)})
        arrays.update({f"shard{c}": shard for c, shard in enumerate(shards)})
        held = {(c, 0): (f"shard{c}", 0, shard.shape[0]) for c, shard in enumerate(shards)}
        crossed, received = {}, {}
        part = depth // groups

        def join(parts):
            views = [arrays[name][first : first + n] for name, first, n in parts]
            return views[0] if len(views) == 1 else jnp.concatenate(views, axis=0)

        def items_of(cs, layer_bits=range(layers), others=range(groups)):
            items = []
            if 0 in layer_bits:
                for r in range(team):
                    described = [(0, r, None if r < 2 else 0)]
                    items.append((described, [(f"layer{r}", 0, c * chunk) for c in cs]))
                for other in range(1, groups):
                    described = [(0, r, other) for r in range(2, team)]
                    items.append((described, [(f"far{other}", 0, c * chunk) for c in cs]))
            for other in others:
                for bits in layer_bits:
                    if bits:
                        described = [(bits, r, other) for r in range(team)]
                        where = [
                            crossed.get((c, bits, other), held[c, bits]) if other else held[c, bits]
                            for c in cs
                        ]
                        items.append((described, [(n, first, 0) for n, first, _ in where]))
            return items

        hardest = [bits for bits in range(layers) if bits.bit_count() == hops]

        def without_last(cs, slow):
            items, rest, late = [], [], []
            for described, parts in items_of(cs):
                if described[0][2] and described[0][0] in slow:
                    name, first, _ = parts[-1]
                    late.append((name, first))
                    rest.append(described)
                    parts = parts[:-1]
                items.append((described, parts))
            late = [(arrays[n], f) for n, f in late if n in arrays]
            return items, rest, late

        for phase in range(1, chunks + hops + 1):
            waited = phase == chunks + hops - 1
            long = {} if waited else {n: arrays.pop(n) for n in LONG if n in arrays}
            if phase < chunks + hops:
                final = {n: arrays.pop(n) for n in [f"phase{phase - 1}from{layers // 2}"] if n in arrays}
                arrays = lax.optimization_barrier(arrays)
                arrays = lax.optimization_barrier({**arrays, **final})
            arrays.update(long)
            sends = []
            ways = {}
            for c in range(chunks):
                for bits in range(1, layers):
                    low = bits & -bits
                    if c + bits.bit_count() == phase:
                        ways.setdefault((0, low), []).append((c, bits, held[c, bits ^ low]))
            if waited:
                sends.append((0, 0, 1, "diagonal", arrays["far_tokens"]))
            for name, listed in received.items():
                for other in range(1, groups):
                    value = tie(arrays[name], *[arrays[n] for n in ("inward",) if n in arrays])
                    sends.append((other, 0, 0, f"{name}_{other}", value))
                    for c, bits in listed:
                        _, first, n = held[c, bits]
                        crossed[c, bits, other] = (f"{name}_{other}", first, n)
            received = {}
            for (other, low), listed in ways.items():
                name = f"phase{phase}from{low}"
                value = join([p for _, _, p in listed])
                sends.append((other, low, 0, name, value))
                received[name] = [(c, bits) for c, bits, _ in listed]
                first = 0
                for c, bits, (_, _, n) in listed:
                    held[c, bits] = (name, first, n)
                    first += n
            if phase == 1:
                sends.append((0, 0, 1, "near", tie(normed, arrays["layer0"])))
                for other in range(1, groups):
                    sends.append((other, 0, 0, f"far{other}", arrays["far"]))
            if phase == hops + 1:
                items, rest, _ = without_last([0], hardest)
                near_tokens = [normed, arrays["near"]]
                arrays["kv_sum"], arrays["kv_left"] = project(
                    place,
                    team,
                    near_tokens,
                    arrays,
                    items,
                    chunk,
                    groups,
                    depth,
                    rest=rest,
                    wanted=True,
                )
                noted = []
                for bits in range(layers):
                    name, start, _ = held[0, bits]
                    noted.append((arrays[name], start + team * part))
                arrays["first"], arrays["count"] = places(place, noted, team * blocks)
            new = {}
            for group_bits, layer_bits, member_bits, name, value in sends:
                new[name] = swap(value, team, group_bits, layer_bits, member_bits)
            arrays.update(new)
            if phase == chunks + hops - 1:
                names = ("normed", "near", "far_tokens", "diagonal")
                team_tokens = [arrays[n] for n in names]
                made = project(
                    place,
                    team,
                    team_tokens[2:],
                    arrays,
                    items_of([0]),
                    chunk,
                    groups,
                    depth,
                    margin,
                    rest=without_last([0], hardest)[1],
                    carried=(arrays["kv_sum"], arrays["kv_left"]),
                )
                arrays.update(zip(("keys_values", "inward", "outward"), made))
        names = ("keys_values", "inward", "outward")
        keys_values, inward, outward = (arrays[n] for n in names)
        items, rest, late = without_last(range(1, chunks), [layers // 2] + hardest)
        *query, begun, left = project(
            place,
            team,
            team_tokens,
            arrays,
            items,
            chunk,
            groups,
            depth,
            rest=rest,
            wanted=True,
        )
        query = (query, begun, left, late)
        first, count = arrays["first"], arrays["count"]
    else:
        (normed,) = normalize(tokens, norm_gain, [rows])
        team_tokens = [normed] + [swap(normed, team, 0, 0, r) for r in range(1, team)]
        stacked = jnp.stack(team_tokens)
        in_order = jnp.concatenate(
            [lax.dynamic_index_in_dim(stacked, member ^ t, 0, False) for t in range(team)]
        )

        def dense(weight, rows_of_tokens):
            whole = lax.all_gather(weight, "seq", axis=0, tiled=True)
            width = weight.shape[1] // team
            own = lax.dynamic_slice_in_dim(whole, member * width, width, 1)
            product = jnp.dot(rows_of_tokens, own, preferred_element_type=jnp.float32)
            return product.astype(jnp.bfloat16)

        keys_values = jnp.concatenate(
            [dense(w_key, in_order), dense(w_value, in_order)], axis=1
        )
        tail, head, odd = keys_values[-margin:], keys_values[:margin], layer % 2 == 1
        inward, outward = jnp.where(odd, head, tail), jnp.where(odd, tail, head)
        query = dense(w_query, stacked.reshape(team * rows, tokens.shape[1]))
        ids = lax.all_gather(passage_blocks, "seq", axis=0, tiled=True)
        mine = jnp.concatenate(
            [
                lax.dynamic_slice_in_dim(ids, (layer * team + (member ^ r)) * blocks, blocks)
                for r in range(team)
            ]
        )

        count = jnp.sum((mine[:, None] == ids[None, :]).astype(jnp.int32), axis=1)
        first = jnp.sum((ids[None, :] < mine[:, None]).astype(jnp.int32), axis=1)
        first = first - layer * team * blocks + (MOST_BLK - 1)
        first, count = first[:, None], count[:, None]

    inner = swap(inward, team, 0, 1, 0)
    outer = swap_outward(outward, team)

    pieces = [None] * team
    for start, end in ((2, team), (0, 2)):
        made = attend(
            first,
            count,
            place,
            query,
            inner,
            keys_values,
            outer,
            block,
            start * blocks,
            rows,
            end - start,
        )
        for r, piece in enumerate(made, start):
            pieces[r] = swap(piece, team, 0, 0, r) if r else piece
    out = jnp.zeros((rows, w_query.shape[1]), jnp.bfloat16)
    for r in [0, *range(2, team), 1]:
        piece = pieces[r]
        out = lax.dynamic_update_slice(out, piece, (0, (member ^ r) * piece.shape[1]))
    return out


def solution(mesh):
    in_specs = (
        P(("groups", "seq"), None),
        P(),
        P("seq", None),
        P("seq", None),
        P("seq", None),
        P(("groups", "seq")),
    )
    out_specs = P(("groups", "seq"), None)
    return jax.shard_map(
        on_device, mesh=mesh, in_specs=in_specs, out_specs=out_specs, check_vma=False
    )
```

```python
import functools

import jax
import jax.numpy as jnp
from jax import lax
from jax.experimental import pallas as pl
from jax.experimental.pallas import tpu as pltpu
from jax.sharding import PartitionSpec as P

HD = 128
MOST_BLK = 7
LANES = 128
NOTES = 16
LONG = ("normed", "far_tokens")
AXES = ("groups", "seq")
LOG2_E = 1.4426950408889634
VMEM_LIMIT = 64 * 1024 * 1024
IN_VMEM = pl.BlockSpec(memory_space=pltpu.VMEM)
IN_SMEM = pl.BlockSpec(memory_space=pltpu.SMEM)
IN_HBM = pl.BlockSpec(memory_space=pltpu.HBM)
PARAMS = pltpu.CompilerParams(vmem_limit_bytes=VMEM_LIMIT)


def cost(flops, size, transcendentals=0):
    return pl.CostEstimate(
        flops=flops, bytes_accessed=size, transcendentals=transcendentals
    )


def swap(value, team, group_bits, layer_bits, member_bits):
    groups, peers = lax.axis_size("groups"), lax.axis_size("seq")
    pairs = []
    for g in range(groups):
        for s in range(peers):
            layer, member = divmod(s, team)
            to = (layer ^ layer_bits) * team + (member ^ member_bits)
            pairs.append((g * peers + s, (g ^ group_bits) * peers + to))
    return lax.ppermute(value, AXES, pairs)


def swap_outward(value, team):
    groups, peers = lax.axis_size("groups"), lax.axis_size("seq")
    pairs = []
    for g in range(groups):
        for s in range(peers):
            to = s + team if s // team % 2 else s - team
            if 0 <= to < peers:
                pairs.append((g * peers + s, g * peers + to))
    return lax.ppermute(value, AXES, pairs)


def tie(value, *others):
    return lax.optimization_barrier((value,) + others)[0] if others else value


def norm_kernel(tokens_ref, gain_ref, *outs):
    first = 0
    for out in outs:
        widened = tokens_ref[first : first + out.shape[0], :].astype(jnp.float32)
        square = jnp.mean(widened * widened, axis=-1, keepdims=True)
        out[...] = (widened * lax.rsqrt(square + 1e-05) * gain_ref[...]).astype(jnp.bfloat16)
        first += out.shape[0]


def normalize(tokens, norm_gain, lengths):
    rows, width = tokens.shape
    return pl.pallas_call(
        norm_kernel,
        out_shape=[jax.ShapeDtypeStruct((n, width), jnp.bfloat16) for n in lengths],
        in_specs=[IN_VMEM] * 2,
        out_specs=[IN_VMEM] * len(lengths),
        compiler_params=PARAMS,
        cost_estimate=cost(6 * rows * width, 4 * rows * width, rows),
        name="normalize",
    )(tokens, norm_gain.reshape(1, width))


def pack_kernel(team, part, notes, count, numbers, *refs):
    group, member = lax.axis_index("groups"), lax.rem(lax.axis_index("seq"), team)
    weights, outs = refs[:count], refs[count : count + team]
    loaded, sems = refs[count + team : -1], refs[-1]
    copies = [
        pltpu.make_async_copy(weight, there, sems.at[i])
        for i, (weight, there) in enumerate(zip(weights, loaded))
    ]
    for copy in copies:
        copy.start()
    if notes:
        row = lax.broadcasted_iota(jnp.int32, (notes, outs[0].shape[1]), 0)
        noted = jnp.zeros((notes, outs[0].shape[1]), jnp.float32)
        for i in range(numbers.shape[0]):
            noted = jnp.where(row == i, numbers[i].astype(jnp.float32), noted)
        noted = noted.astype(jnp.bfloat16)
        for out in outs:
            out[out.shape[0] - notes :, :] = noted
    column = 0
    for copy, weight in zip(copies, loaded):
        copy.wait()
        width = weight.shape[1] // team
        for r, out in enumerate(outs):
            length = out.shape[0] - notes
            first = 0 if r < 2 else pl.multiple_of(group * part, part)
            columns = pl.ds(pl.multiple_of((member ^ r) * width, width), width)
            out[:length, column : column + width] = weight[pl.ds(first, length), columns]
        column += width


def pack(numbers, weights, team, groups, notes=0):
    depth = weights[0].shape[0]
    width = sum(weight.shape[1] for weight in weights) // team
    lengths = [depth if r < 2 else depth // groups for r in range(team)]
    return pl.pallas_call(
        functools.partial(pack_kernel, team, depth // groups, notes, len(weights)),
        out_shape=[
            jax.ShapeDtypeStruct((length + notes, width), jnp.bfloat16)
            for length in lengths
        ],
        in_specs=[IN_SMEM] + [IN_HBM] * len(weights),
        out_specs=[IN_VMEM] * team,
        scratch_shapes=[pltpu.VMEM(w.shape, w.dtype) for w in weights]
        + [pltpu.SemaphoreType.DMA((len(weights),))],
        compiler_params=PARAMS,
        cost_estimate=cost(0, 4 * team * depth * width),
        name="pack",
    )(numbers, *weights)


def shards_kernel(team, part, blocks, place, *refs):
    ins, shards, far = refs[:team], refs[team:-1], refs[-1]
    mine = pl.ds(pl.multiple_of(place[0] * part, part), part)
    for r, ref in enumerate(ins):
        rows = mine if r < 2 else pl.ds(0, part)
        column = 0
        for shard in shards:
            width = shard.shape[1]
            shard[r * part : (r + 1) * part, :] = ref[rows, column : column + width]
            column += width
        if r >= 2:
            far[(r - 2) * part : (r - 1) * part, :] = ref[rows, :]
    if not blocks:
        return
    noted_in = shards[0]
    row = lax.broadcasted_iota(jnp.int32, (NOTES, noted_in.shape[1]), 0)
    noted = jnp.zeros((NOTES, noted_in.shape[1]), jnp.float32)
    for r, ref in enumerate(ins):
        held = ref[ref.shape[0] - NOTES :, : noted_in.shape[1]].astype(jnp.float32)
        for i in range(blocks):
            noted = jnp.where(row == r * blocks + i, held[i : i + 1, :], noted)
    noted_in[team * part :, :] = noted.astype(jnp.bfloat16)


def make_shards(place, packed, moved, widths, depth, groups, blocks=0):
    part, width = depth // groups, packed.shape[1]
    team = 1 + len(moved)
    shapes = [(team * part + (NOTES if blocks and not i else 0), w) for i, w in enumerate(widths)]
    shapes.append(((team - 2) * part, width))
    return pl.pallas_call(
        functools.partial(shards_kernel, team, part, blocks),
        out_shape=[jax.ShapeDtypeStruct(shape, jnp.bfloat16) for shape in shapes],
        in_specs=[IN_SMEM] + [IN_VMEM] * team,
        out_specs=[IN_VMEM] * len(shapes),
        compiler_params=PARAMS,
        cost_estimate=cost(0, 6 * team * part * width),
        name="shards",
    )(place, packed, *moved)


def project_kernel(items, counts, chunk, margin, rest, team, groups, depth, place, *refs):
    held, arrays, wanted, carried = counts
    sources, refs = refs[:held], refs[held:]
    stored, refs = refs[:arrays], refs[arrays:]
    begun, refs = refs[: 2 * carried], refs[2 * carried :]
    outs, (tokens, weights, total, lefts, token_sems, sems) = refs[:-6], refs[-6:]
    part = depth // groups
    span = 2 * sources[0].shape[0]
    if carried:
        near = pl.ds(0, span)
        pairs = [(begun[0], total.at[near]), (begun[1], lefts)]
        carries = [
            pltpu.make_async_copy(*pair, sems.at[sems.shape[0] - 2 + i])
            for i, pair in enumerate(pairs)
        ]
        for copy in carries:
            copy.start()
    group, layer, member = place[0], place[1], place[2]
    layer_wide = team * depth
    layers = sorted({described[0][0] for described, _ in items})
    plan, offset, copies, token_copies = [], 0, 0, 0
    for layer_bits in layers:
        loads, matched, row = [], [], 0
        first = pl.multiple_of((layer ^ layer_bits) * layer_wide, LANES)
        for ref in sources:
            here = pl.ds(first, layer_wide)
            there = tokens.at[pl.ds(row, ref.shape[0]), here]
            loads.append(
                pltpu.make_async_copy(ref.at[:, here], there, token_sems.at[token_copies])
            )
            row += ref.shape[0]
            token_copies += 1
        for described, parts in items:
            if described[0][0] != layer_bits:
                continue
            deep = sum(depth if bits[2] is None else part for bits in described)
            for c, (source, first, column) in enumerate(parts):
                loads.append(
                    pltpu.make_async_copy(
                        stored[source].at[pl.ds(first, deep), pl.ds(column, chunk)],
                        weights.at[pl.ds(offset, deep), pl.ds(c * chunk, chunk)],
                        sems.at[copies],
                    )
                )
                copies += 1
            matched.append((described, offset, deep, len(parts) * chunk))
            offset += deep
        for copy in loads:
            copy.start()
        plan.append((loads, matched))

    def columns_of(own, described):
        lefts = []
        for layer_bits, member_bits, group_bits in described:
            owner = (layer ^ layer_bits) * team + (member ^ member_bits)
            first, wide = owner * depth, depth
            if group_bits is not None:
                first, wide = first + (group ^ group_bits) * part, part
            lefts.append(tokens[own, pl.ds(pl.multiple_of(first, LANES), wide)])
        return lefts[0] if len(lefts) == 1 else jnp.concatenate(lefts, axis=1)

    shift = span if carried else 0
    if carried:
        for copy in carries:
            copy.wait()
    for step, (loads, matched) in enumerate(plan):
        for copy in loads:
            copy.wait()
        for half in range(tokens.shape[0] // span):
            own = pl.ds(half * span, span)
            to = pl.ds(half * span + shift, span)
            for i, (described, offset, deep, wide) in enumerate(matched):
                right = weights[pl.ds(offset, deep), :wide]
                term = jnp.dot(
                    columns_of(own, described), right, preferred_element_type=jnp.float32
                )
                if i == 0 and step == 0:
                    total[to, :wide] = term
                else:
                    total[to, :wide] += term
        if carried:
            column = 0
            for described in rest:
                for other, offset, deep, wide in matched:
                    if other == described:
                        total[near, :wide] += jnp.dot(
                            lefts[:, column : column + deep],
                            weights[pl.ds(offset, deep), :wide],
                            preferred_element_type=jnp.float32,
                        )
                column += sum(depth if bits[2] is None else part for bits in described)
    if wanted:
        column = 0
        for described in rest:
            left = columns_of(pl.ds(0, tokens.shape[0]), described)
            outs[-1][:, column : column + left.shape[1]] = left
            column += left.shape[1]
    rows = total.shape[0] // team
    chunks = total.shape[1] // chunk
    for c in range(chunks):
        columns = slice(c * chunk, (c + 1) * chunk)
        if rest and not carried and c + 1 == chunks:
            outs[c][...] = total[:, columns]
            continue
        for r in range(team):
            first = r * rows
            if c == 0 and margin is not None:
                first = pl.multiple_of((member ^ r) * rows, rows)
            made = total[r * rows : (r + 1) * rows, columns]
            outs[c][pl.ds(first, rows), :] = made.astype(jnp.bfloat16)
    if margin is not None:
        late, odd = total.shape[0] - margin, lax.rem(layer, 2)
        for out, first in ((outs[chunks], (1 - odd) * late), (outs[chunks + 1], odd * late)):
            out[...] = outs[0][pl.ds(pl.multiple_of(first, LANES), margin), :]


def project(
    place,
    team,
    tokens,
    arrays,
    items,
    chunk,
    groups,
    depth,
    margin=None,
    rest=(),
    wanted=False,
    carried=(),
):
    taken, width = sum(value.shape[0] for value in tokens), tokens[0].shape[1]
    count = taken + (carried[0].shape[0] if carried else 0)
    chunks = max(len(parts) for _, parts in items)
    names = sorted({name for _, parts in items for name, _, _ in parts})
    items = [
        (described, [(names.index(n), first, column) for n, first, column in parts])
        for described, parts in items
        if parts
    ]

    def deep_of(listed):
        return sum(depth // (1 if b[2] is None else groups) for d in listed for b in d)

    deep = deep_of([described for described, _ in items])
    copies = sum(len(parts) for _, parts in items)
    lacking = bool(rest) and not carried
    kinds = [jnp.bfloat16] * (chunks - lacking) + [jnp.float32] * lacking
    shapes = [jax.ShapeDtypeStruct((count, chunk), kind) for kind in kinds]
    if margin is not None:
        shapes += [jax.ShapeDtypeStruct((margin, chunk), jnp.bfloat16)] * 2
    if wanted:
        shapes.append(jax.ShapeDtypeStruct((count, deep_of(rest)), jnp.bfloat16))
    return pl.pallas_call(
        functools.partial(
            project_kernel,
            items,
            (len(tokens), len(names), wanted, bool(carried)),
            chunk,
            margin,
            rest,
            team,
            groups,
            depth,
        ),
        out_shape=shapes,
        in_specs=[IN_SMEM] + [IN_HBM] * (len(tokens) + len(names) + len(carried)),
        out_specs=[IN_VMEM] * len(shapes),
        scratch_shapes=[
            pltpu.VMEM((taken, width), jnp.bfloat16),
            pltpu.VMEM((deep, chunks * chunk), jnp.bfloat16),
            pltpu.VMEM((count, chunks * chunk), jnp.float32),
            pltpu.VMEM(carried[1].shape if carried else (NOTES, LANES), jnp.bfloat16),
            pltpu.SemaphoreType.DMA((len(tokens) * width // (team * depth),)),
            pltpu.SemaphoreType.DMA((copies + len(carried),)),
        ],
        compiler_params=PARAMS,
        cost_estimate=cost(
            2 * taken * deep * chunks * chunk,
            2 * chunks * chunk * (count + deep) + 2 * taken * width,
        ),
        name="project",
    )(place, *tokens, *[arrays[name] for name in names], *carried)


def places_kernel(blocks, firsts, place, *refs):
    ins, (first, count), (held, sems) = refs[:-4], refs[-4:-2], refs[-2:]
    copies = []
    for i, (ref, start) in enumerate(zip(ins, firsts)):
        there = held.at[pl.ds(i * NOTES, NOTES)]
        copies.append(pltpu.make_async_copy(ref.at[pl.ds(start, NOTES)], there, sems.at[i]))
        copies[-1].start()
    for copy in copies:
        copy.wait()
    ids = held[:, :LANES].astype(jnp.float32)
    mine = ids[:NOTES]
    same, less = jnp.zeros_like(mine), jnp.zeros_like(mine)
    for i in range(len(ins)):
        for k in range(blocks):
            other = ids[i * NOTES + k : i * NOTES + k + 1]
            same += (other == mine).astype(jnp.float32)
            less += (other < mine).astype(jnp.float32)
    count[...] = same.astype(jnp.int32)
    first[...] = less.astype(jnp.int32) - place[1] * blocks + (MOST_BLK - 1)


def places(place, noted, blocks):
    shape = jax.ShapeDtypeStruct((NOTES, LANES), jnp.int32)
    width = noted[0][0].shape[1]
    first, count = pl.pallas_call(
        functools.partial(places_kernel, blocks, [start for _, start in noted]),
        out_shape=[shape] * 2,
        in_specs=[IN_SMEM] + [IN_HBM] * len(noted),
        out_specs=[IN_VMEM] * 2,
        scratch_shapes=[
            pltpu.VMEM((len(noted) * NOTES, width), jnp.bfloat16),
            pltpu.SemaphoreType.DMA((len(noted),)),
        ],
        compiler_params=PARAMS,
        cost_estimate=cost(0, 4 * NOTES * width * len(noted)),
        name="places",
    )(place, *[array for array, _ in noted])
    return first, count


def attend_kernel(
    base, block, deep, firsts, first_ref, count_ref, place, inner, own, outer, *refs
):
    outs, (window, query) = refs[:-2][-(len(refs) - 2 - firsts[0]) :], refs[-2:]
    ins = refs[: firsts[0]]
    per_out = outs[0].shape[0] // block
    total_blocks = per_out * len(outs)
    column = 0
    for ref in ins[: firsts[0] - (2 + len(firsts[1]) if deep else 0)]:
        query[:, column : column + ref.shape[1]] = ref[...]
        column += ref.shape[1]
    if deep:
        begun, left, *weights = ins[firsts[0] - 2 - len(firsts[1]) :]
        total = begun[...]
        for i, (weight, start) in enumerate(zip(weights, firsts[1])):
            total += jnp.dot(
                left[:, i * deep : (i + 1) * deep],
                weight[start : start + deep, :],
                preferred_element_type=jnp.float32,
            )
        query[:, column:] = total.astype(jnp.bfloat16)
    margin, odd = inner.shape[0], lax.rem(place[1], 2)
    window[margin : margin + own.shape[0], :] = own[...]

    @pl.when(odd == 0)
    def _():
        window[:margin, :] = outer[...]
        window[margin + own.shape[0] :, :] = inner[...]

    @pl.when(odd == 1)
    def _():
        window[:margin, :] = inner[...]
        window[margin + own.shape[0] :, :] = outer[...]

    heads = query.shape[1] // HD
    span = MOST_BLK * block

    def place_of(b):
        return pl.ds(pl.multiple_of(first_ref[base + b, 0] * block, block), span)

    def score(b):
        rows = pl.ds(b * block, block)
        stacked = jnp.concatenate(
            [query[rows, h * HD : (h + 1) * HD] for h in range(heads)], axis=0
        )
        return lax.dot_general(
            window[place_of(b), :HD],
            stacked,
            (((1,), (1,)), ((), ())),
            preferred_element_type=jnp.float32,
        )

    scores = score(0)
    for b in range(total_blocks):
        upcoming = score(b + 1) if b + 1 < total_blocks else None
        scores = jnp.concatenate(
            [scores[:block]]
            + [
                jnp.where(count_ref[base + b, 0] > k, scores[k * block : (k + 1) * block], -1e30)
                for k in range(1, MOST_BLK)
            ],
            axis=0,
        )
        row_max = jnp.max(scores, axis=0, keepdims=True)
        weights = jnp.exp2((scores - row_max) * (HD ** (-0.5) * LOG2_E))
        row_total = jnp.sum(weights, axis=0, keepdims=True)
        mixed = lax.dot_general(
            window[place_of(b), HD:],
            weights.astype(jnp.bfloat16),
            (((0,), (0,)), ((), ())),
            preferred_element_type=jnp.float32,
        )
        mixed = mixed / row_total
        out = outs[b // per_out]
        rows = pl.ds((b % per_out) * block, block)
        for h in range(heads):
            turned = mixed[:, h * block : (h + 1) * block].T
            out[rows, h * HD : (h + 1) * HD] = turned.astype(jnp.bfloat16)
        scores = upcoming


def attend(first, count, place, query, inner, own, outer, block, base, rows, parts):
    if isinstance(query, tuple):
        done, begun, left, late = query
        ins = [*done, begun, left] + [array for array, _ in late]
        firsts = (len(ins), [start for _, start in late])
        deep = left.shape[1] // len(late)
        columns = sum(value.shape[1] for value in done) + begun.shape[1]
    else:
        ins, firsts, deep, columns = [query], (1, []), 0, query.shape[1]
    span = 2 * inner.shape[0] + own.shape[0]
    size = parts * rows
    by_rows = [value.shape[0] == own.shape[0] and i < len(ins) - len(firsts[1])
               for i, value in enumerate(ins)]
    specs = [
        pl.BlockSpec((size, value.shape[1]), lambda i: (base * block // size, 0))
        if cut else IN_VMEM
        for value, cut in zip(ins, by_rows)
    ]
    return pl.pallas_call(
        functools.partial(attend_kernel, base, block, deep, firsts),
        out_shape=[jax.ShapeDtypeStruct((rows, columns), jnp.bfloat16)] * parts,
        grid=(1,),
        in_specs=[IN_SMEM] * 3 + [IN_VMEM] * 3 + specs,
        out_specs=[IN_VMEM] * parts,
        scratch_shapes=[
            pltpu.VMEM((span, own.shape[1]), jnp.bfloat16),
            pltpu.VMEM((parts * rows, columns), jnp.bfloat16),
        ],
        compiler_params=PARAMS,
        cost_estimate=cost(
            4 * parts * rows * MOST_BLK * block * columns,
            4 * rows * columns + 2 * span * own.shape[1],
            parts * rows * MOST_BLK * block * (columns // HD),
        ),
        name="attend",
    )(first, count, place, inner, own, outer, *ins)


def assemble_kernel(place, *refs):
    pieces, out = refs[:-1], refs[-1]
    for r, piece in enumerate(pieces):
        width = piece.shape[1]
        first = pl.multiple_of((place[2] ^ r) * width, width)
        out[:, pl.ds(first, width)] = piece[...]


def assemble(place, pieces):
    rows, width = pieces[0].shape
    return pl.pallas_call(
        assemble_kernel,
        out_shape=jax.ShapeDtypeStruct((rows, width * len(pieces)), jnp.bfloat16),
        in_specs=[IN_SMEM] + [IN_VMEM] * len(pieces),
        out_specs=IN_VMEM,
        compiler_params=PARAMS,
        cost_estimate=cost(0, 4 * rows * width * len(pieces)),
        name="assemble",
    )(place, *pieces)


def on_device(tokens, norm_gain, w_query, w_key, w_value, passage_blocks):
    groups, peers = lax.axis_size("groups"), lax.axis_size("seq")
    team = w_key.shape[1] // HD
    layers = peers // team
    depth = w_key.shape[0]
    rows = tokens.shape[0]
    blocks = passage_blocks.shape[0]
    block = rows // blocks
    index = lax.axis_index("seq")
    group, layer, member = lax.axis_index("groups"), index // team, index % team
    place = jnp.stack([group, layer, member]).astype(jnp.int32)
    widths = [2 * HD] * ((w_key.shape[1] + w_value.shape[1] + w_query.shape[1]) // (2 * HD * team))
    margin = (MOST_BLK - 1) * block

    if depth // groups % LANES == 0 and team * blocks <= NOTES:
        chunk = 2 * HD
        weights = [w_key, w_value, w_query]
        packed = pack(passage_blocks, weights, team, groups, NOTES)
        moved = [swap(packed[r], team, 0, 0, r) for r in range(1, team)]
        (normed,) = normalize(tie(tokens, packed[0]), norm_gain, [rows])
        *shards, far = make_shards(
            tie(place, normed), packed[0], moved, widths, depth, groups, blocks
        )

        chunks = len(shards)
        hops = max(bits.bit_count() for bits in range(layers))
        arrays = {"layer0": packed[0], "far": far, "normed": normed}
        arrays["far_tokens"] = swap(tie(normed, *moved[1:]), team, 0, 0, 2)
        arrays.update({f"layer{r}": value for r, value in enumerate(moved, 1)})
        arrays.update({f"shard{c}": shard for c, shard in enumerate(shards)})
        held = {(c, 0): (f"shard{c}", 0, shard.shape[0]) for c, shard in enumerate(shards)}
        crossed, received = {}, {}
        part = depth // groups

        def join(parts):
            views = [arrays[name][first : first + n] for name, first, n in parts]
            return views[0] if len(views) == 1 else jnp.concatenate(views, axis=0)

        def items_of(cs, layer_bits=range(layers), others=range(groups)):
            items = []
            if 0 in layer_bits:
                for r in range(team):
                    described = [(0, r, None if r < 2 else 0)]
                    items.append((described, [(f"layer{r}", 0, c * chunk) for c in cs]))
                for other in range(1, groups):
                    described = [(0, r, other) for r in range(2, team)]
                    items.append((described, [(f"far{other}", 0, c * chunk) for c in cs]))
            for other in others:
                for bits in layer_bits:
                    if bits:
                        described = [(bits, r, other) for r in range(team)]
                        where = [
                            crossed.get((c, bits, other), held[c, bits]) if other else held[c, bits]
                            for c in cs
                        ]
                        items.append((described, [(n, first, 0) for n, first, _ in where]))
            return items

        hardest = [bits for bits in range(layers) if bits.bit_count() == hops]

        def without_last(cs, slow):
            items, rest, late = [], [], []
            for described, parts in items_of(cs):
                if described[0][2] and described[0][0] in slow:
                    name, first, _ = parts[-1]
                    late.append((name, first))
                    rest.append(described)
                    parts = parts[:-1]
                items.append((described, parts))
            late = [(arrays[n], f) for n, f in late if n in arrays]
            return items, rest, late

        for phase in range(1, chunks + hops + 1):
            waited = phase == chunks + hops - 1
            long = {} if waited else {n: arrays.pop(n) for n in LONG if n in arrays}
            if phase < chunks + hops:
                final = {n: arrays.pop(n) for n in [f"phase{phase - 1}from{layers // 2}"] if n in arrays}
                arrays = lax.optimization_barrier(arrays)
                arrays = lax.optimization_barrier({**arrays, **final})
            arrays.update(long)
            sends = []
            ways = {}
            for c in range(chunks):
                for bits in range(1, layers):
                    low = bits & -bits
                    if c + bits.bit_count() == phase:
                        ways.setdefault((0, low), []).append((c, bits, held[c, bits ^ low]))
            if waited:
                sends.append((0, 0, 1, "diagonal", arrays["far_tokens"]))
            for name, listed in received.items():
                for other in range(1, groups):
                    value = tie(arrays[name], *[arrays[n] for n in ("inward",) if n in arrays])
                    sends.append((other, 0, 0, f"{name}_{other}", value))
                    for c, bits in listed:
                        _, first, n = held[c, bits]
                        crossed[c, bits, other] = (f"{name}_{other}", first, n)
            received = {}
            for (other, low), listed in ways.items():
                name = f"phase{phase}from{low}"
                value = join([p for _, _, p in listed])
                sends.append((other, low, 0, name, value))
                received[name] = [(c, bits) for c, bits, _ in listed]
                first = 0
                for c, bits, (_, _, n) in listed:
                    held[c, bits] = (name, first, n)
                    first += n
            if phase == 1:
                sends.append((0, 0, 1, "near", tie(normed, arrays["layer0"])))
                for other in range(1, groups):
                    sends.append((other, 0, 0, f"far{other}", arrays["far"]))
            if phase == hops + 1:
                items, rest, _ = without_last([0], hardest)
                near_tokens = [normed, arrays["near"]]
                arrays["kv_sum"], arrays["kv_left"] = project(
                    place,
                    team,
                    near_tokens,
                    arrays,
                    items,
                    chunk,
                    groups,
                    depth,
                    rest=rest,
                    wanted=True,
                )
                noted = []
                for bits in range(layers):
                    name, start, _ = held[0, bits]
                    noted.append((arrays[name], start + team * part))
                arrays["first"], arrays["count"] = places(place, noted, team * blocks)
            new = {}
            for group_bits, layer_bits, member_bits, name, value in sends:
                new[name] = swap(value, team, group_bits, layer_bits, member_bits)
            arrays.update(new)
            if phase == chunks + hops - 1:
                names = ("normed", "near", "far_tokens", "diagonal")
                team_tokens = [arrays[n] for n in names]
                made = project(
                    place,
                    team,
                    team_tokens[2:],
                    arrays,
                    items_of([0]),
                    chunk,
                    groups,
                    depth,
                    margin,
                    rest=without_last([0], hardest)[1],
                    carried=(arrays["kv_sum"], arrays["kv_left"]),
                )
                arrays.update(zip(("keys_values", "inward", "outward"), made))
        names = ("keys_values", "inward", "outward")
        keys_values, inward, outward = (arrays[n] for n in names)
        items, rest, late = without_last(range(1, chunks), [layers // 2] + hardest)
        *query, begun, left = project(
            place,
            team,
            team_tokens,
            arrays,
            items,
            chunk,
            groups,
            depth,
            rest=rest,
            wanted=True,
        )
        query = (query, begun, left, late)
        first, count = arrays["first"], arrays["count"]
    else:
        (normed,) = normalize(tokens, norm_gain, [rows])
        team_tokens = [normed] + [swap(normed, team, 0, 0, r) for r in range(1, team)]
        stacked = jnp.stack(team_tokens)
        in_order = jnp.concatenate(
            [lax.dynamic_index_in_dim(stacked, member ^ t, 0, False) for t in range(team)]
        )

        def dense(weight, rows_of_tokens):
            whole = lax.all_gather(weight, "seq", axis=0, tiled=True)
            width = weight.shape[1] // team
            own = lax.dynamic_slice_in_dim(whole, member * width, width, 1)
            product = jnp.dot(rows_of_tokens, own, preferred_element_type=jnp.float32)
            return product.astype(jnp.bfloat16)

        keys_values = jnp.concatenate(
            [dense(w_key, in_order), dense(w_value, in_order)], axis=1
        )
        tail, head, odd = keys_values[-margin:], keys_values[:margin], layer % 2 == 1
        inward, outward = jnp.where(odd, head, tail), jnp.where(odd, tail, head)
        query = dense(w_query, stacked.reshape(team * rows, tokens.shape[1]))
        ids = lax.all_gather(passage_blocks, "seq", axis=0, tiled=True)
        mine = jnp.concatenate(
            [
                lax.dynamic_slice_in_dim(ids, (layer * team + (member ^ r)) * blocks, blocks)
                for r in range(team)
            ]
        )

        count = jnp.sum((mine[:, None] == ids[None, :]).astype(jnp.int32), axis=1)
        first = jnp.sum((ids[None, :] < mine[:, None]).astype(jnp.int32), axis=1)
        first = first - layer * team * blocks + (MOST_BLK - 1)
        first, count = first[:, None], count[:, None]

    inner = swap(inward, team, 0, 1, 0)
    outer = swap_outward(outward, team)

    pieces = [None] * team
    for start, end in ((2, team), (0, 2)):
        made = attend(
            first,
            count,
            place,
            query,
            inner,
            keys_values,
            outer,
            block,
            start * blocks,
            rows,
            end - start,
        )
        for r, piece in enumerate(made, start):
            pieces[r] = swap(piece, team, 0, 0, r) if r else piece
    pieces[2:] = lax.optimization_barrier(pieces[2:])
    pieces = lax.optimization_barrier(pieces)
    return assemble(place, pieces)


def solution(mesh):
    in_specs = (
        P(("groups", "seq"), None),
        P(),
        P("seq", None),
        P("seq", None),
        P("seq", None),
        P(("groups", "seq")),
    )
    out_specs = P(("groups", "seq"), None)
    return jax.shard_map(
        on_device, mesh=mesh, in_specs=in_specs, out_specs=out_specs, check_vma=False
    )
```

```python
import functools

import jax
import jax.numpy as jnp
from jax import lax
from jax.experimental import pallas as pl
from jax.experimental.pallas import tpu as pltpu
from jax.sharding import PartitionSpec as P

HD = 128
MOST_BLK = 7
LANES = 128
NOTES = 16
LONG = ("normed", "far_tokens")
AXES = ("groups", "seq")
LOG2_E = 1.4426950408889634
VMEM_LIMIT = 64 * 1024 * 1024
IN_VMEM = pl.BlockSpec(memory_space=pltpu.VMEM)
IN_SMEM = pl.BlockSpec(memory_space=pltpu.SMEM)
IN_HBM = pl.BlockSpec(memory_space=pltpu.HBM)
PARAMS = pltpu.CompilerParams(vmem_limit_bytes=VMEM_LIMIT)


def cost(flops, size, transcendentals=0):
    return pl.CostEstimate(
        flops=flops, bytes_accessed=size, transcendentals=transcendentals
    )


def swap(value, team, group_bits, layer_bits, member_bits):
    groups, peers = lax.axis_size("groups"), lax.axis_size("seq")
    pairs = []
    for g in range(groups):
        for s in range(peers):
            layer, member = divmod(s, team)
            to = (layer ^ layer_bits) * team + (member ^ member_bits)
            pairs.append((g * peers + s, (g ^ group_bits) * peers + to))
    return lax.ppermute(value, AXES, pairs)


def swap_outward(value, team):
    groups, peers = lax.axis_size("groups"), lax.axis_size("seq")
    pairs = []
    for g in range(groups):
        for s in range(peers):
            to = s + team if s // team % 2 else s - team
            if 0 <= to < peers:
                pairs.append((g * peers + s, g * peers + to))
    return lax.ppermute(value, AXES, pairs)


def tie(value, *others):
    return lax.optimization_barrier((value,) + others)[0] if others else value


def norm_kernel(tokens_ref, gain_ref, *outs):
    first = 0
    for out in outs:
        widened = tokens_ref[first : first + out.shape[0], :].astype(jnp.float32)
        square = jnp.mean(widened * widened, axis=-1, keepdims=True)
        out[...] = (widened * lax.rsqrt(square + 1e-05) * gain_ref[...]).astype(jnp.bfloat16)
        first += out.shape[0]


def normalize(tokens, norm_gain, lengths):
    rows, width = tokens.shape
    return pl.pallas_call(
        norm_kernel,
        out_shape=[jax.ShapeDtypeStruct((n, width), jnp.bfloat16) for n in lengths],
        in_specs=[IN_VMEM] * 2,
        out_specs=[IN_VMEM] * len(lengths),
        compiler_params=PARAMS,
        cost_estimate=cost(6 * rows * width, 4 * rows * width, rows),
        name="normalize",
    )(tokens, norm_gain.reshape(1, width))


def pack_kernel(team, part, notes, count, numbers, *refs):
    group, member = lax.axis_index("groups"), lax.rem(lax.axis_index("seq"), team)
    weights, outs = refs[:count], refs[count : count + team]
    loaded, sems = refs[count + team : -1], refs[-1]
    copies = [
        pltpu.make_async_copy(weight, there, sems.at[i])
        for i, (weight, there) in enumerate(zip(weights, loaded))
    ]
    for copy in copies:
        copy.start()
    if notes:
        row = lax.broadcasted_iota(jnp.int32, (notes, outs[0].shape[1]), 0)
        noted = jnp.zeros((notes, outs[0].shape[1]), jnp.float32)
        for i in range(numbers.shape[0]):
            noted = jnp.where(row == i, numbers[i].astype(jnp.float32), noted)
        noted = noted.astype(jnp.bfloat16)
        for out in outs:
            out[out.shape[0] - notes :, :] = noted
    column = 0
    for copy, weight in zip(copies, loaded):
        copy.wait()
        width = weight.shape[1] // team
        for r, out in enumerate(outs):
            length = out.shape[0] - notes
            first = 0 if r < 2 else pl.multiple_of(group * part, part)
            columns = pl.ds(pl.multiple_of((member ^ r) * width, width), width)
            out[:length, column : column + width] = weight[pl.ds(first, length), columns]
        column += width


def pack(numbers, weights, team, groups, notes=0):
    depth = weights[0].shape[0]
    width = sum(weight.shape[1] for weight in weights) // team
    lengths = [depth if r < 2 else depth // groups for r in range(team)]
    return pl.pallas_call(
        functools.partial(pack_kernel, team, depth // groups, notes, len(weights)),
        out_shape=[
            jax.ShapeDtypeStruct((length + notes, width), jnp.bfloat16)
            for length in lengths
        ],
        in_specs=[IN_SMEM] + [IN_HBM] * len(weights),
        out_specs=[IN_VMEM] * team,
        scratch_shapes=[pltpu.VMEM(w.shape, w.dtype) for w in weights]
        + [pltpu.SemaphoreType.DMA((len(weights),))],
        compiler_params=PARAMS,
        cost_estimate=cost(0, 4 * team * depth * width),
        name="pack",
    )(numbers, *weights)


def shards_kernel(team, part, blocks, place, *refs):
    ins, shards, far = refs[:team], refs[team:-1], refs[-1]
    mine = pl.ds(pl.multiple_of(place[0] * part, part), part)
    for r, ref in enumerate(ins):
        rows = mine if r < 2 else pl.ds(0, part)
        column = 0
        for shard in shards:
            width = shard.shape[1]
            shard[r * part : (r + 1) * part, :] = ref[rows, column : column + width]
            column += width
        if r >= 2:
            far[(r - 2) * part : (r - 1) * part, :] = ref[rows, :]
    if not blocks:
        return
    noted_in = shards[0]
    row = lax.broadcasted_iota(jnp.int32, (NOTES, noted_in.shape[1]), 0)
    noted = jnp.zeros((NOTES, noted_in.shape[1]), jnp.float32)
    for r, ref in enumerate(ins):
        held = ref[ref.shape[0] - NOTES :, : noted_in.shape[1]].astype(jnp.float32)
        for i in range(blocks):
            noted = jnp.where(row == r * blocks + i, held[i : i + 1, :], noted)
    noted_in[team * part :, :] = noted.astype(jnp.bfloat16)


def make_shards(place, packed, moved, widths, depth, groups, blocks=0):
    part, width = depth // groups, packed.shape[1]
    team = 1 + len(moved)
    shapes = [(team * part + (NOTES if blocks and not i else 0), w) for i, w in enumerate(widths)]
    shapes.append(((team - 2) * part, width))
    return pl.pallas_call(
        functools.partial(shards_kernel, team, part, blocks),
        out_shape=[jax.ShapeDtypeStruct(shape, jnp.bfloat16) for shape in shapes],
        in_specs=[IN_SMEM] + [IN_VMEM] * team,
        out_specs=[IN_VMEM] * len(shapes),
        compiler_params=PARAMS,
        cost_estimate=cost(0, 6 * team * part * width),
        name="shards",
    )(place, packed, *moved)


def project_kernel(items, counts, chunk, margin, rest, team, groups, depth, place, *refs):
    held, arrays, wanted, carried = counts
    sources, refs = refs[:held], refs[held:]
    stored, refs = refs[:arrays], refs[arrays:]
    begun, refs = refs[: 2 * carried], refs[2 * carried :]
    outs, (tokens, weights, total, lefts, token_sems, sems) = refs[:-6], refs[-6:]
    part = depth // groups
    span = 2 * sources[0].shape[0]
    if carried:
        near = pl.ds(0, span)
        pairs = [(begun[0], total.at[near]), (begun[1], lefts)]
        carries = [
            pltpu.make_async_copy(*pair, sems.at[sems.shape[0] - 2 + i])
            for i, pair in enumerate(pairs)
        ]
        for copy in carries:
            copy.start()
    group, layer, member = place[0], place[1], place[2]
    layer_wide = team * depth
    layers = sorted({described[0][0] for described, _ in items})
    plan, offset, copies, token_copies = [], 0, 0, 0
    for layer_bits in layers:
        loads, matched, row = [], [], 0
        first = pl.multiple_of((layer ^ layer_bits) * layer_wide, LANES)
        for ref in sources:
            here = pl.ds(first, layer_wide)
            there = tokens.at[pl.ds(row, ref.shape[0]), here]
            loads.append(
                pltpu.make_async_copy(ref.at[:, here], there, token_sems.at[token_copies])
            )
            row += ref.shape[0]
            token_copies += 1
        for described, parts in items:
            if described[0][0] != layer_bits:
                continue
            deep = sum(depth if bits[2] is None else part for bits in described)
            for c, (source, first, column) in enumerate(parts):
                loads.append(
                    pltpu.make_async_copy(
                        stored[source].at[pl.ds(first, deep), pl.ds(column, chunk)],
                        weights.at[pl.ds(offset, deep), pl.ds(c * chunk, chunk)],
                        sems.at[copies],
                    )
                )
                copies += 1
            matched.append((described, offset, deep, len(parts) * chunk))
            offset += deep
        for copy in loads:
            copy.start()
        plan.append((loads, matched))

    def columns_of(own, described):
        lefts = []
        for layer_bits, member_bits, group_bits in described:
            owner = (layer ^ layer_bits) * team + (member ^ member_bits)
            first, wide = owner * depth, depth
            if group_bits is not None:
                first, wide = first + (group ^ group_bits) * part, part
            lefts.append(tokens[own, pl.ds(pl.multiple_of(first, LANES), wide)])
        return lefts[0] if len(lefts) == 1 else jnp.concatenate(lefts, axis=1)

    shift = span if carried else 0
    if carried:
        for copy in carries:
            copy.wait()
    for step, (loads, matched) in enumerate(plan):
        for copy in loads:
            copy.wait()
        for half in range(tokens.shape[0] // span):
            own = pl.ds(half * span, span)
            to = pl.ds(half * span + shift, span)
            for i, (described, offset, deep, wide) in enumerate(matched):
                right = weights[pl.ds(offset, deep), :wide]
                term = jnp.dot(
                    columns_of(own, described), right, preferred_element_type=jnp.float32
                )
                if i == 0 and step == 0:
                    total[to, :wide] = term
                else:
                    total[to, :wide] += term
        if carried:
            column = 0
            for described in rest:
                for other, offset, deep, wide in matched:
                    if other == described:
                        total[near, :wide] += jnp.dot(
                            lefts[:, column : column + deep],
                            weights[pl.ds(offset, deep), :wide],
                            preferred_element_type=jnp.float32,
                        )
                column += sum(depth if bits[2] is None else part for bits in described)
    if wanted:
        column = 0
        for described in rest:
            left = columns_of(pl.ds(0, tokens.shape[0]), described)
            outs[-1][:, column : column + left.shape[1]] = left
            column += left.shape[1]
    rows = total.shape[0] // team
    chunks = total.shape[1] // chunk
    for c in range(chunks):
        columns = slice(c * chunk, (c + 1) * chunk)
        if rest and not carried and c + 1 == chunks:
            outs[c][...] = total[:, columns]
            continue
        for r in range(team):
            first = r * rows
            if c == 0 and margin is not None:
                first = pl.multiple_of((member ^ r) * rows, rows)
            made = total[r * rows : (r + 1) * rows, columns]
            outs[c][pl.ds(first, rows), :] = made.astype(jnp.bfloat16)
    if margin is not None:
        late, odd = total.shape[0] - margin, lax.rem(layer, 2)
        for out, first in ((outs[chunks], (1 - odd) * late), (outs[chunks + 1], odd * late)):
            out[...] = outs[0][pl.ds(pl.multiple_of(first, LANES), margin), :]


def project(
    place,
    team,
    tokens,
    arrays,
    items,
    chunk,
    groups,
    depth,
    margin=None,
    rest=(),
    wanted=False,
    carried=(),
):
    taken, width = sum(value.shape[0] for value in tokens), tokens[0].shape[1]
    count = taken + (carried[0].shape[0] if carried else 0)
    chunks = max(len(parts) for _, parts in items)
    names = sorted({name for _, parts in items for name, _, _ in parts})
    items = [
        (described, [(names.index(n), first, column) for n, first, column in parts])
        for described, parts in items
        if parts
    ]

    def deep_of(listed):
        return sum(depth // (1 if b[2] is None else groups) for d in listed for b in d)

    deep = deep_of([described for described, _ in items])
    copies = sum(len(parts) for _, parts in items)
    lacking = bool(rest) and not carried
    kinds = [jnp.bfloat16] * (chunks - lacking) + [jnp.float32] * lacking
    shapes = [jax.ShapeDtypeStruct((count, chunk), kind) for kind in kinds]
    if margin is not None:
        shapes += [jax.ShapeDtypeStruct((margin, chunk), jnp.bfloat16)] * 2
    if wanted:
        shapes.append(jax.ShapeDtypeStruct((count, deep_of(rest)), jnp.bfloat16))
    return pl.pallas_call(
        functools.partial(
            project_kernel,
            items,
            (len(tokens), len(names), wanted, bool(carried)),
            chunk,
            margin,
            rest,
            team,
            groups,
            depth,
        ),
        out_shape=shapes,
        in_specs=[IN_SMEM] + [IN_HBM] * (len(tokens) + len(names) + len(carried)),
        out_specs=[IN_VMEM] * len(shapes),
        scratch_shapes=[
            pltpu.VMEM((taken, width), jnp.bfloat16),
            pltpu.VMEM((deep, chunks * chunk), jnp.bfloat16),
            pltpu.VMEM((count, chunks * chunk), jnp.float32),
            pltpu.VMEM(carried[1].shape if carried else (NOTES, LANES), jnp.bfloat16),
            pltpu.SemaphoreType.DMA((len(tokens) * width // (team * depth),)),
            pltpu.SemaphoreType.DMA((copies + len(carried),)),
        ],
        compiler_params=PARAMS,
        cost_estimate=cost(
            2 * taken * deep * chunks * chunk,
            2 * chunks * chunk * (count + deep) + 2 * taken * width,
        ),
        name="project",
    )(place, *tokens, *[arrays[name] for name in names], *carried)


def places_kernel(blocks, firsts, place, *refs):
    ins, (first, count), (held, sems) = refs[:-4], refs[-4:-2], refs[-2:]
    copies = []
    for i, (ref, start) in enumerate(zip(ins, firsts)):
        there = held.at[pl.ds(i * NOTES, NOTES)]
        copies.append(pltpu.make_async_copy(ref.at[pl.ds(start, NOTES)], there, sems.at[i]))
        copies[-1].start()
    for copy in copies:
        copy.wait()
    ids = held[:, :LANES].astype(jnp.float32)
    mine = ids[:NOTES]
    same, less = jnp.zeros_like(mine), jnp.zeros_like(mine)
    for i in range(len(ins)):
        for k in range(blocks):
            other = ids[i * NOTES + k : i * NOTES + k + 1]
            same += (other == mine).astype(jnp.float32)
            less += (other < mine).astype(jnp.float32)
    count[...] = same.astype(jnp.int32)
    first[...] = less.astype(jnp.int32) - place[1] * blocks + (MOST_BLK - 1)


def places(place, noted, blocks):
    shape = jax.ShapeDtypeStruct((NOTES, LANES), jnp.int32)
    width = noted[0][0].shape[1]
    first, count = pl.pallas_call(
        functools.partial(places_kernel, blocks, [start for _, start in noted]),
        out_shape=[shape] * 2,
        in_specs=[IN_SMEM] + [IN_HBM] * len(noted),
        out_specs=[IN_VMEM] * 2,
        scratch_shapes=[
            pltpu.VMEM((len(noted) * NOTES, width), jnp.bfloat16),
            pltpu.SemaphoreType.DMA((len(noted),)),
        ],
        compiler_params=PARAMS,
        cost_estimate=cost(0, 4 * NOTES * width * len(noted)),
        name="places",
    )(place, *[array for array, _ in noted])
    return first, count


def attend_kernel(
    base, block, deep, firsts, first_ref, count_ref, place, inner, own, outer, *refs
):
    outs, (window, query) = refs[:-2][-(len(refs) - 2 - firsts[0]) :], refs[-2:]
    ins = refs[: firsts[0]]
    per_out = outs[0].shape[0] // block
    total_blocks = per_out * len(outs)
    column = 0
    for ref in ins[: firsts[0] - (2 + len(firsts[1]) if deep else 0)]:
        query[:, column : column + ref.shape[1]] = ref[...]
        column += ref.shape[1]
    if deep:
        begun, left, *weights = ins[firsts[0] - 2 - len(firsts[1]) :]
        total = begun[...]
        for i, (weight, start) in enumerate(zip(weights, firsts[1])):
            total += jnp.dot(
                left[:, i * deep : (i + 1) * deep],
                weight[start : start + deep, :],
                preferred_element_type=jnp.float32,
            )
        query[:, column:] = total.astype(jnp.bfloat16)
    margin, odd = inner.shape[0], lax.rem(place[1], 2)
    window[margin : margin + own.shape[0], :] = own[...]

    @pl.when(odd == 0)
    def _():
        window[:margin, :] = outer[...]
        window[margin + own.shape[0] :, :] = inner[...]

    @pl.when(odd == 1)
    def _():
        window[:margin, :] = inner[...]
        window[margin + own.shape[0] :, :] = outer[...]

    heads = query.shape[1] // HD
    span = MOST_BLK * block

    def place_of(b):
        return pl.ds(pl.multiple_of(first_ref[base + b, 0] * block, block), span)

    def score(b):
        rows = pl.ds(b * block, block)
        stacked = jnp.concatenate(
            [query[rows, h * HD : (h + 1) * HD] for h in range(heads)], axis=0
        )
        return lax.dot_general(
            window[place_of(b), :HD],
            stacked,
            (((1,), (1,)), ((), ())),
            preferred_element_type=jnp.float32,
        )

    scores = score(0)
    for b in range(total_blocks):
        upcoming = score(b + 1) if b + 1 < total_blocks else None
        scores = jnp.concatenate(
            [scores[:block]]
            + [
                jnp.where(count_ref[base + b, 0] > k, scores[k * block : (k + 1) * block], -1e30)
                for k in range(1, MOST_BLK)
            ],
            axis=0,
        )
        row_max = jnp.max(scores, axis=0, keepdims=True)
        weights = jnp.exp2((scores - row_max) * (HD ** (-0.5) * LOG2_E))
        row_total = jnp.sum(weights, axis=0, keepdims=True)
        mixed = lax.dot_general(
            window[place_of(b), HD:],
            weights.astype(jnp.bfloat16),
            (((0,), (0,)), ((), ())),
            preferred_element_type=jnp.float32,
        )
        mixed = mixed / row_total
        out = outs[b // per_out]
        rows = pl.ds((b % per_out) * block, block)
        for h in range(heads):
            turned = mixed[:, h * block : (h + 1) * block].T
            out[rows, h * HD : (h + 1) * HD] = turned.astype(jnp.bfloat16)
        scores = upcoming


def attend(first, count, place, query, inner, own, outer, block, base, rows, parts):
    if isinstance(query, tuple):
        done, begun, left, late = query
        ins = [*done, begun, left] + [array for array, _ in late]
        firsts = (len(ins), [start for _, start in late])
        deep = left.shape[1] // len(late)
        columns = sum(value.shape[1] for value in done) + begun.shape[1]
    else:
        ins, firsts, deep, columns = [query], (1, []), 0, query.shape[1]
    span = 2 * inner.shape[0] + own.shape[0]
    size = parts * rows
    by_rows = [value.shape[0] == own.shape[0] and i < len(ins) - len(firsts[1])
               for i, value in enumerate(ins)]
    specs = [
        pl.BlockSpec((size, value.shape[1]), lambda i: (base * block // size, 0))
        if cut else IN_VMEM
        for value, cut in zip(ins, by_rows)
    ]
    return pl.pallas_call(
        functools.partial(attend_kernel, base, block, deep, firsts),
        out_shape=[jax.ShapeDtypeStruct((rows, columns), jnp.bfloat16)] * parts,
        grid=(1,),
        in_specs=[IN_SMEM] * 3 + [IN_VMEM] * 3 + specs,
        out_specs=[IN_VMEM] * parts,
        scratch_shapes=[
            pltpu.VMEM((span, own.shape[1]), jnp.bfloat16),
            pltpu.VMEM((parts * rows, columns), jnp.bfloat16),
        ],
        compiler_params=PARAMS,
        cost_estimate=cost(
            4 * parts * rows * MOST_BLK * block * columns,
            4 * rows * columns + 2 * span * own.shape[1],
            parts * rows * MOST_BLK * block * (columns // HD),
        ),
        name="attend",
    )(first, count, place, inner, own, outer, *ins)


def assemble_kernel(place, *refs):
    pieces, out = refs[:-1], refs[-1]
    for r, piece in enumerate(pieces):
        width = piece.shape[1]
        first = pl.multiple_of((place[2] ^ r) * width, width)
        out[:, pl.ds(first, width)] = piece[...]


def assemble(place, pieces):
    rows, width = pieces[0].shape
    return pl.pallas_call(
        assemble_kernel,
        out_shape=jax.ShapeDtypeStruct((rows, width * len(pieces)), jnp.bfloat16),
        in_specs=[IN_SMEM] + [IN_VMEM] * len(pieces),
        out_specs=IN_VMEM,
        compiler_params=PARAMS,
        cost_estimate=cost(0, 4 * rows * width * len(pieces)),
        name="assemble",
    )(place, *pieces)


def on_device(tokens, norm_gain, w_query, w_key, w_value, passage_blocks):
    groups, peers = lax.axis_size("groups"), lax.axis_size("seq")
    team = w_key.shape[1] // HD
    layers = peers // team
    depth = w_key.shape[0]
    rows = tokens.shape[0]
    blocks = passage_blocks.shape[0]
    block = rows // blocks
    index = lax.axis_index("seq")
    group, layer, member = lax.axis_index("groups"), index // team, index % team
    place = jnp.stack([group, layer, member]).astype(jnp.int32)
    widths = [2 * HD] * ((w_key.shape[1] + w_value.shape[1] + w_query.shape[1]) // (2 * HD * team))
    margin = (MOST_BLK - 1) * block

    if depth // groups % LANES == 0 and team * blocks <= NOTES:
        chunk = 2 * HD
        weights = [w_key, w_value, w_query]
        packed = pack(passage_blocks, weights, team, groups, NOTES)
        moved = [swap(packed[r], team, 0, 0, r) for r in range(1, team)]
        (normed,) = normalize(tie(tokens, packed[0]), norm_gain, [rows])
        *shards, far = make_shards(
            tie(place, normed), packed[0], moved, widths, depth, groups, blocks
        )

        chunks = len(shards)
        hops = max(bits.bit_count() for bits in range(layers))
        arrays = {"layer0": packed[0], "far": far, "normed": normed}
        arrays["far_tokens"] = swap(tie(normed, *moved[1:]), team, 0, 0, 2)
        arrays.update({f"layer{r}": value for r, value in enumerate(moved, 1)})
        arrays.update({f"shard{c}": shard for c, shard in enumerate(shards)})
        held = {(c, 0): (f"shard{c}", 0, shard.shape[0]) for c, shard in enumerate(shards)}
        crossed, received = {}, {}
        part = depth // groups

        def join(parts):
            views = [arrays[name][first : first + n] for name, first, n in parts]
            return views[0] if len(views) == 1 else jnp.concatenate(views, axis=0)

        def items_of(cs, layer_bits=range(layers), others=range(groups)):
            items = []
            if 0 in layer_bits:
                for r in range(team):
                    described = [(0, r, None if r < 2 else 0)]
                    items.append((described, [(f"layer{r}", 0, c * chunk) for c in cs]))
                for other in range(1, groups):
                    described = [(0, r, other) for r in range(2, team)]
                    items.append((described, [(f"far{other}", 0, c * chunk) for c in cs]))
            for other in others:
                for bits in layer_bits:
                    if bits:
                        described = [(bits, r, other) for r in range(team)]
                        where = [
                            crossed.get((c, bits, other), held[c, bits]) if other else held[c, bits]
                            for c in cs
                        ]
                        items.append((described, [(n, first, 0) for n, first, _ in where]))
            return items

        hardest = [bits for bits in range(layers) if bits.bit_count() == hops]

        def without_last(cs, slow):
            items, rest, late = [], [], []
            for described, parts in items_of(cs):
                if described[0][2] and described[0][0] in slow:
                    name, first, _ = parts[-1]
                    late.append((name, first))
                    rest.append(described)
                    parts = parts[:-1]
                items.append((described, parts))
            late = [(arrays[n], f) for n, f in late if n in arrays]
            return items, rest, late

        for phase in range(1, chunks + hops + 1):
            waited = phase == chunks + hops - 1
            long = {} if waited else {n: arrays.pop(n) for n in LONG if n in arrays}
            if phase < chunks + hops:
                final = {n: arrays.pop(n) for n in [f"phase{phase - 1}from{layers // 2}", f"phase{phase - 1}from1"] if n in arrays}
                arrays = lax.optimization_barrier(arrays)
                arrays = lax.optimization_barrier({**arrays, **final})
            arrays.update(long)
            sends = []
            ways = {}
            for c in range(chunks):
                for bits in range(1, layers):
                    low = bits & -bits
                    if c + bits.bit_count() == phase:
                        ways.setdefault((0, low), []).append((c, bits, held[c, bits ^ low]))
            if waited:
                sends.append((0, 0, 1, "diagonal", arrays["far_tokens"]))
            for name, listed in received.items():
                for other in range(1, groups):
                    value = tie(arrays[name], *[arrays[n] for n in ("inward",) if n in arrays])
                    sends.append((other, 0, 0, f"{name}_{other}", value))
                    for c, bits in listed:
                        _, first, n = held[c, bits]
                        crossed[c, bits, other] = (f"{name}_{other}", first, n)
            received = {}
            for (other, low), listed in ways.items():
                name = f"phase{phase}from{low}"
                value = join([p for _, _, p in listed])
                sends.append((other, low, 0, name, value))
                received[name] = [(c, bits) for c, bits, _ in listed]
                first = 0
                for c, bits, (_, _, n) in listed:
                    held[c, bits] = (name, first, n)
                    first += n
            if phase == 1:
                sends.append((0, 0, 1, "near", tie(normed, arrays["layer0"])))
                for other in range(1, groups):
                    sends.append((other, 0, 0, f"far{other}", arrays["far"]))
            if phase == hops + 1:
                items, rest, _ = without_last([0], hardest)
                near_tokens = [normed, arrays["near"]]
                arrays["kv_sum"], arrays["kv_left"] = project(
                    place,
                    team,
                    near_tokens,
                    arrays,
                    items,
                    chunk,
                    groups,
                    depth,
                    rest=rest,
                    wanted=True,
                )
                noted = []
                for bits in range(layers):
                    name, start, _ = held[0, bits]
                    noted.append((arrays[name], start + team * part))
                arrays["first"], arrays["count"] = places(place, noted, team * blocks)
            new = {}
            for group_bits, layer_bits, member_bits, name, value in sends:
                new[name] = swap(value, team, group_bits, layer_bits, member_bits)
            arrays.update(new)
            if phase == chunks + hops - 1:
                names = ("normed", "near", "far_tokens", "diagonal")
                team_tokens = [arrays[n] for n in names]
                made = project(
                    place,
                    team,
                    team_tokens[2:],
                    arrays,
                    items_of([0]),
                    chunk,
                    groups,
                    depth,
                    margin,
                    rest=without_last([0], hardest)[1],
                    carried=(arrays["kv_sum"], arrays["kv_left"]),
                )
                arrays.update(zip(("keys_values", "inward", "outward"), made))
        names = ("keys_values", "inward", "outward")
        keys_values, inward, outward = (arrays[n] for n in names)
        items, rest, late = without_last(range(1, chunks), [layers // 2] + hardest)
        *query, begun, left = project(
            place,
            team,
            team_tokens,
            arrays,
            items,
            chunk,
            groups,
            depth,
            rest=rest,
            wanted=True,
        )
        query = (query, begun, left, late)
        first, count = arrays["first"], arrays["count"]
    else:
        (normed,) = normalize(tokens, norm_gain, [rows])
        team_tokens = [normed] + [swap(normed, team, 0, 0, r) for r in range(1, team)]
        stacked = jnp.stack(team_tokens)
        in_order = jnp.concatenate(
            [lax.dynamic_index_in_dim(stacked, member ^ t, 0, False) for t in range(team)]
        )

        def dense(weight, rows_of_tokens):
            whole = lax.all_gather(weight, "seq", axis=0, tiled=True)
            width = weight.shape[1] // team
            own = lax.dynamic_slice_in_dim(whole, member * width, width, 1)
            product = jnp.dot(rows_of_tokens, own, preferred_element_type=jnp.float32)
            return product.astype(jnp.bfloat16)

        keys_values = jnp.concatenate(
            [dense(w_key, in_order), dense(w_value, in_order)], axis=1
        )
        tail, head, odd = keys_values[-margin:], keys_values[:margin], layer % 2 == 1
        inward, outward = jnp.where(odd, head, tail), jnp.where(odd, tail, head)
        query = dense(w_query, stacked.reshape(team * rows, tokens.shape[1]))
        ids = lax.all_gather(passage_blocks, "seq", axis=0, tiled=True)
        mine = jnp.concatenate(
            [
                lax.dynamic_slice_in_dim(ids, (layer * team + (member ^ r)) * blocks, blocks)
                for r in range(team)
            ]
        )

        count = jnp.sum((mine[:, None] == ids[None, :]).astype(jnp.int32), axis=1)
        first = jnp.sum((ids[None, :] < mine[:, None]).astype(jnp.int32), axis=1)
        first = first - layer * team * blocks + (MOST_BLK - 1)
        first, count = first[:, None], count[:, None]

    inner = swap(inward, team, 0, 1, 0)
    outer = swap_outward(outward, team)

    pieces = [None] * team
    for start, end in ((2, team), (0, 2)):
        made = attend(
            first,
            count,
            place,
            query,
            inner,
            keys_values,
            outer,
            block,
            start * blocks,
            rows,
            end - start,
        )
        for r, piece in enumerate(made, start):
            pieces[r] = swap(piece, team, 0, 0, r) if r else piece
    pieces[2:] = lax.optimization_barrier(pieces[2:])
    pieces = lax.optimization_barrier(pieces)
    return assemble(place, pieces)


def solution(mesh):
    in_specs = (
        P(("groups", "seq"), None),
        P(),
        P("seq", None),
        P("seq", None),
        P("seq", None),
        P(("groups", "seq")),
    )
    out_specs = P(("groups", "seq"), None)
    return jax.shard_map(
        on_device, mesh=mesh, in_specs=in_specs, out_specs=out_specs, check_vma=False
    )
```
